1024 devices in a mesh: gx: 16 (over z, core), gy: 64 (over x, y).
Axes of the slice: x: 8, y: 8, z: 8, core: 2. Of those that a mesh axis runs over, the one named last changes fastest.
Arguments:
- populations: float32 [19, 256, 256, 128], P(None, 'gx', 'gy'), as said below
- vert_base: int32 [3, 524288], P(None, ('gx', 'gy')), may hold values from 0 to 255, as said below
- vert_frac: float32 [3, 524288], P(None, ('gx', 'gy')), may hold values from 0 to 0.999
- edges: int32 [2, 1572864], P(None, ('gx', 'gy')), may hold values from 0 to 511, as said below
- stiffness: float32 [1572864], P(('gx', 'gy')), may hold values from 0.05 to 0.5
- rest: float32 [3, 1572864], P(None, ('gx', 'gy')), may hold values from -3 to 3
Outputs:
- fresh: float32 [19, 256, 256, 128], P(None, 'gx', 'gy')
- vertex_velocity: float32 [3, 524288], P(None, ('gx', 'gy'))
The draws below stay inside these ranges and needn't reach their ends.
Inputs may be any that keep to these rules, and one draw needn't show every extreme that they name: `vert_base`: the first coordinate lies below 256, the second below 256, the third below 128. The vertices are in blocks of 512, block k belonging to the k-th device in the order gx then gy; a vertex's first coordinate lies in that device's 16 cells along x, its second in its 4 cells along y. Each run of 128 vertices of a block lies in a box of 4 x 4 x 4 cells, periodic in z. `edges`: edge e belongs to block e // 1536; its two entries are distinct indices within that block's 512 vertices, both in the same run of 128 vertices. `populations`: every entry lies between 0.6 and 1.4 times the lattice weight of its direction.
All inputs are finite; a program needn't handle non-finite values.
Results may differ from the reference program's by a relative error of at most 0.000078.
Values sent between devices are 32-bit elements; how exact they have to be, the bound alone decides.
No kernel may reach another device: no remote copies, remote signals or barrier semaphores. Data moves between devices by JAX's collectives and lax.ppermute only.
A program may use at most 32 MiB of HBM per device.

```python
import math
import jax
import jax.numpy as jnp
import numpy as np
from jax import lax

CX = 16
CY = 4
NZ = 128
VERT_DEV = 512
TILE = 128
NX = 256
NY = 256
VERTS = 524288
EDGE_DEV = 1536
EDGES = 1572864


table_weights = np.array([1.0 / 3.0] + [1.0 / 18.0] * 6 + [1.0 / 36.0] * 12, np.float32)


def draw_populations(key, part):
    shape = (19, NX, NY, NZ)
    noise = jax.random.uniform(key, shape, jnp.float32, -0.38, 0.38)
    weights = jnp.asarray(table_weights, jnp.float32)[:, None, None, None]
    return weights * (1.0 + noise)


def draw_vert_base(key, part):
    tile_count = VERTS // TILE
    column_count = NY // CY
    vertex = jnp.arange(VERTS, dtype=jnp.int32)
    block = vertex // VERT_DEV
    tile = vertex // TILE
    tile_x = jax.random.randint(jax.random.fold_in(key, 11), (tile_count,), 0, CX - 3)
    tile_y = jax.random.randint(jax.random.fold_in(key, 12), (tile_count,), 0, CY - 3)
    tile_z = jax.random.randint(jax.random.fold_in(key, 13), (tile_count,), 0, NZ)
    spread = jax.random.randint(jax.random.fold_in(key, 14), (3, VERTS), 0, 4)
    first = block // column_count * CX + tile_x[tile] + spread[0]
    second = block % column_count * CY + tile_y[tile] + spread[1]
    third = (tile_z[tile] + spread[2]) % NZ
    return jnp.stack([first, second, third]).astype(jnp.int32)


def draw_edges(key, part):
    local = jnp.arange(EDGES, dtype=jnp.int32) % EDGE_DEV
    group = local // (3 * TILE)
    start = jax.random.randint(jax.random.fold_in(key, 21), (EDGES,), 0, TILE)
    stride = jax.random.randint(jax.random.fold_in(key, 22), (EDGES,), 1, TILE)
    first = group * TILE + start
    second = group * TILE + (start + stride) % TILE
    return jnp.stack([first, second]).astype(jnp.int32)


def levels(rng, extent, pieces, smallest, largest):
    gain = 1.0
    for dim, shards_of in pieces:
        steps = jax.random.uniform(jax.random.fold_in(jax.random.fold_in(rng, 6), dim), (shards_of,), jnp.float32, smallest / len(pieces), largest / len(pieces))
        gain = gain * jnp.repeat(jnp.exp(steps), extent[dim] // shards_of).reshape((-1,) + (1,) * (len(extent) - 1 - dim))
    return gain


def centred(stream_key, shape, scale, most, pieces=(), kind=jnp.bfloat16):
    factor_of = levels(stream_key, shape, pieces, -0.22, 0.18) if pieces else 1.0
    drawn = jax.random.normal(stream_key, shape, jnp.float32) * scale * factor_of
    return jnp.minimum(jnp.maximum(drawn, -most), most).astype(kind)


def setup_inputs(seed: int = 0) -> dict:
    streams_of = jax.random.split(jax.random.key(seed), 7)
    return {
        "populations": draw_populations(jax.random.fold_in(streams_of[6], 71), 0),
        "vert_base": draw_vert_base(jax.random.fold_in(streams_of[6], 71), 0),
        "vert_frac": jnp.clip(0.999 * jax.random.uniform(streams_of[2], (3, VERTS), jnp.float32) ** levels(streams_of[2], (3, VERTS), ((1, 1024),), -0.2, 0.2), 0.0, 0.999),
        "edges": draw_edges(jax.random.fold_in(streams_of[6], 71), 0),
        "stiffness": jnp.clip(jnp.exp(math.log(0.5) - 2.3025851 * jax.random.uniform(streams_of[4], (EDGES,), jnp.float32) ** levels(streams_of[4], (EDGES,), ((0, 1024),), -0.2, 0.2)), 0.05, 0.5),
        "rest": centred(streams_of[5], (3, EDGES), 0.5, 3.0, ((1, 1024),), jnp.float32),
    }


lattice_speeds = [(0, 0, 0), (1, 0, 0), (-1, 0, 0), (0, 1, 0), (0, -1, 0), (0, 0, 1), (0, 0, -1), (1, 1, 0), (-1, -1, 0), (1, -1, 0), (-1, 1, 0), (1, 0, 1), (-1, 0, -1), (1, 0, -1), (-1, 0, 1), (0, 1, 1), (0, -1, -1), (0, 1, -1), (0, -1, 1)]
lattice_weights = [1.0 / 3.0] + [1.0 / 18.0] * 6 + [1.0 / 36.0] * 12
relax_time = 0.9

def outer_weight(r):
    return (5.0 - 2.0 * r - jnp.sqrt(-7.0 + 12.0 * r - 4.0 * r * r)) / 8.0

def inner_weight(r):
    return (3.0 - 2.0 * r + jnp.sqrt(1.0 + 4.0 * r - 4.0 * r * r)) / 8.0

def kernel_weights(frac):
    return jnp.stack([outer_weight(1.0 + frac), inner_weight(frac), inner_weight(1.0 - frac), outer_weight(2.0 - frac)])

def collide(popul, force):
    speeds = jnp.asarray(lattice_speeds, jnp.float32)
    weights = jnp.asarray(lattice_weights, jnp.float32)[:, None, None, None]
    high = lax.Precision.HIGHEST
    density = lax.optimization_barrier(jnp.sum(popul, axis=0))
    moment = jnp.tensordot(speeds.T, popul, axes=1, precision=high)
    velocity = (moment + 0.5 * force) / density
    along = jnp.tensordot(speeds, velocity, axes=1, precision=high)
    square = lax.optimization_barrier(jnp.sum(velocity * velocity, axis=0))
    balance = weights * density * (1.0 + 3.0 * along + 4.5 * along * along - 1.5 * square)
    push = jnp.tensordot(speeds, force, axes=1, precision=high)
    work = lax.optimization_barrier(jnp.sum(velocity * force, axis=0))
    source = (1.0 - 0.5 / relax_time) * weights * (3.0 * (push - work) + 9.0 * along * push)
    post = popul - (popul - balance) / relax_time + source
    return (post, velocity)

def reference(populations, vert_base, vert_frac, edges, stiffness, rest):
    position = vert_base.astype(jnp.float32) + vert_frac
    offset = jnp.arange(EDGES, dtype=jnp.int32) // EDGE_DEV * VERT_DEV
    first = edges[0] + offset
    second = edges[1] + offset
    stretch = stiffness[None, :] * (position[:, second] - position[:, first] - rest)
    membrane = jnp.zeros((3, VERTS), jnp.float32).at[:, first].add(stretch).at[:, second].add(-stretch)
    kernel = kernel_weights(vert_frac)
    grid = jnp.zeros((3, NX, NY, NZ), jnp.float32)
    cells = []
    for kx in range(4):
        for ky in range(4):
            for kz in range(4):
                index_x = (vert_base[0] - 1 + kx) % NX
                index_y = (vert_base[1] - 1 + ky) % NY
                index_z = (vert_base[2] - 1 + kz) % NZ
                weight = kernel[kx, 0] * kernel[ky, 1] * kernel[kz, 2]
                cells.append((index_x, index_y, index_z, weight))
                grid = grid.at[:, index_x, index_y, index_z].add(membrane * weight[None, :])
    post, velocity = collide(populations, grid)
    rows = []
    for q in range(19):
        shift = lattice_speeds[q]
        rows.append(jnp.roll(post[q], shift, axis=(0, 1, 2)))
    fresh = jnp.stack(rows)
    sampled = jnp.zeros((3, VERTS), jnp.float32)
    for index_x, index_y, index_z, weight in cells:
        sampled = sampled + velocity[:, index_x, index_y, index_z] * weight[None, :]
    return (fresh, sampled)
```

```python
import jax
import jax.numpy as jnp
from jax import lax
from jax.experimental import pallas as pl
from jax.experimental.pallas import tpu as pltpu
from jax.sharding import PartitionSpec as P

lattice_speeds = [
    (0, 0, 0),
    (1, 0, 0),
    (-1, 0, 0),
    (0, 1, 0),
    (0, -1, 0),
    (0, 0, 1),
    (0, 0, -1),
    (1, 1, 0),
    (-1, -1, 0),
    (1, -1, 0),
    (-1, 1, 0),
    (1, 0, 1),
    (-1, 0, -1),
    (1, 0, -1),
    (-1, 0, 1),
    (0, 1, 1),
    (0, -1, -1),
    (0, 1, -1),
    (0, -1, 1),
]
lattice_weights = [1.0 / 3.0] + [1.0 / 18.0] * 6 + [1.0 / 36.0] * 12
relax_time = 0.9

f32 = jnp.float32
bf16 = jnp.bfloat16

WX, WY, NZ = 16, 4, 128
CELLS = WX * WY
VERTS, TILE, EDGES = 512, 128, 1536
SX, SY = 24, 7

UP_Y = [q for q in range(19) if lattice_speeds[q][1] == 1]
DOWN_Y = [q for q in range(19) if lattice_speeds[q][1] == -1]
UP_X = [q for q in range(19) if lattice_speeds[q][0] == 1]
DOWN_X = [q for q in range(19) if lattice_speeds[q][0] == -1]

FORCE_ROWS = 9 * WX + 3 * 16
UP_ROWS = FORCE_ROWS + 4 * WX + 5 * WX
DOWN_ROWS = FORCE_ROWS + 8 * WX + 5 * WX
RIGHT_ROWS = 3 * 24 + 32 + 24
LEFT_ROWS = 3 * 24 + 2 * 32 + 24


def outer_weight(r):
    return (5.0 - 2.0 * r - jnp.sqrt(-7.0 + 12.0 * r - 4.0 * r * r)) / 8.0


def inner_weight(r):
    return (3.0 - 2.0 * r + jnp.sqrt(1.0 + 4.0 * r - 4.0 * r * r)) / 8.0


def halves(value):
    high = value.astype(bf16)
    low = (value - high.astype(f32)).astype(bf16)
    return high, low


def along_last(a, b):
    return lax.dot_general(a, b, (((1,), (1,)), ((), ())), preferred_element_type=f32)


def iota(shape, dim):
    return lax.broadcasted_iota(jnp.int32, shape, dim)


def edge_forces(base, frac, edges, stiffness, rest):
    head = edges[0:1]
    tail = edges[1:2]
    run = head >> 7
    local = iota((TILE, EDGES), 0)
    plus = local == (tail & (TILE - 1))
    minus = local == (head & (TILE - 1))
    signed = jnp.where(plus, 1.0, jnp.where(minus, -1.0, 0.0)).astype(bf16)
    whole = base.astype(f32)
    high, low = halves(frac)
    blank = jnp.zeros((5, TILE), f32)
    pieces = []
    for part in (whole, high.astype(f32), low.astype(f32)):
        for t in range(4):
            pieces += [part[:, t * TILE : (t + 1) * TILE], blank]
    stacked = jnp.concatenate(pieces, axis=0).astype(bf16)
    found = jnp.dot(stacked, signed, preferred_element_type=f32)
    found = found[0:32] + found[32:64] + found[64:96]
    apart = jnp.zeros((8, EDGES), f32)
    for t in range(4):
        apart = apart + jnp.where(run == t, found[8 * t : 8 * t + 8], 0.0)
    stretch = stiffness * (apart[0:3] - rest)
    high, low = halves(stretch)
    blank = jnp.zeros((5, EDGES), f32)
    pieces = []
    for part in (high.astype(f32), low.astype(f32)):
        for t in range(4):
            pieces += [jnp.where(run == t, part, 0.0), blank]
    stacked = jnp.concatenate(pieces, axis=0).astype(bf16)
    pulled = along_last(stacked, signed)
    pulled = pulled[0:32] + pulled[32:64]
    return jnp.concatenate([-pulled[8 * t : 8 * t + 3] for t in range(4)], axis=1)


def spread_kernel(
    pop, base, frac, edges, stiffness, rest, force, moment, plane_out, high_out, low_out, edge_out, up, down
):
    membrane = edge_forces(base[...], frac[...], edges[...], stiffness[...], rest[...])
    part = frac[...]
    kernel = [
        outer_weight(1.0 + part),
        inner_weight(part),
        inner_weight(1.0 - part),
        outer_weight(2.0 - part),
    ]
    cell = base[...]

    def columns(rows, offset, dim):
        total = jnp.zeros((rows, VERTS), f32)
        for step in range(4):
            total = jnp.where(offset == step, kernel[step][dim : dim + 1], total)
        return total

    slot = iota((SX, VERTS), 0)
    slot = jnp.where(slot == SX - 1, -1, slot)
    along_x = columns(SX, slot - (cell[0:1] & (WX - 1)) + 1, 0)
    slab = iota((8, VERTS), 0)
    along_y = columns(8, slab - (cell[1:2] & (WY - 1)), 1)
    depth = iota((NZ, VERTS), 0)
    along_z = columns(NZ, (depth - cell[2:3] + 1) & (NZ - 1), 2)
    plane = jnp.concatenate([along_x * along_y[y : y + 1] for y in range(SY)], axis=0)
    plane_out[...] = plane
    z_high, z_low = halves(along_z)
    high_out[...] = z_high
    low_out[...] = z_low

    density = pop[0:CELLS]
    moments = [None, None, None]
    for q in range(1, 19):
        value = pop[q * CELLS : (q + 1) * CELLS]
        density = density + value
        for d in range(3):
            c = lattice_speeds[q][d]
            if c:
                if moments[d] is None:
                    moments[d] = value if c > 0 else -value
                else:
                    moments[d] = moments[d] + value if c > 0 else moments[d] - value
    moment[0:CELLS] = density
    for d in range(3):
        moment[(d + 1) * CELLS : (d + 2) * CELLS] = moments[d]

    plane_high, plane_low = halves(plane)
    for c in range(3):
        load_high, load_low = halves(along_z * membrane[c : c + 1])
        result = (
            along_last(plane_high, load_high)
            + along_last(plane_low, load_high)
            + along_last(plane_high, load_low)
        )
        for y in range(SY):
            force[(y * 3 + c) * SX : (y * 3 + c + 1) * SX] = result[y * SX : (y + 1) * SX]

    def strips(out, slab, rows, dirs, edge_row):
        at = 0
        for k in range(9):
            out[at : at + WX] = force[(slab * 3 + k) * SX : (slab * 3 + k) * SX + WX]
            at += WX
        for x in (16, 17, 23):
            out[at : at + 9] = force[pl.ds(slab * 3 * SX + x, 9, stride=SX), :]
            at += 16
        for y in rows:
            for q in range(4):
                out[at : at + WX] = moment[pl.ds(q * CELLS + y, WX, stride=WY), :]
                at += WX
        for q in dirs:
            out[at : at + WX] = pop[pl.ds(q * CELLS + edge_row, WX, stride=WY), :]
            at += WX

    strips(up, 4, (3,), UP_Y, 3)
    strips(down, 0, (0, 1), DOWN_Y, 0)
    for k, q in enumerate(UP_X):
        edge_out[k * 4 : k * 4 + 4] = pop[q * CELLS + 60 : q * CELLS + 64]
    for k, q in enumerate(DOWN_X):
        edge_out[24 + k * 4 : 24 + k * 4 + 4] = pop[q * CELLS : q * CELLS + 4]


def merge_kernel(force_in, moment, edge, below, above, force, right, left):
    def outer(block, slab):
        for k in range(9):
            row = (slab * 3 + k) * SX
            force[row : row + WX] = force_in[row : row + WX] + block[k * WX : k * WX + WX]
        for n, x in enumerate((16, 17, 23)):
            rows = pl.ds(slab * 3 * SX + x, 9, stride=SX)
            at = 9 * WX + 16 * n
            force[rows, :] = force_in[rows, :] + block[at : at + 9]

    for k in range(9, 12):
        force[k * SX : (k + 1) * SX] = force_in[k * SX : (k + 1) * SX]
    for slab in (0, 4):
        for k in range(9):
            row = (slab * 3 + k) * SX + 16
            force[row : row + 8] = force_in[row : row + 8]
    outer(below, 0)
    outer(above, 4)

    def outgoing(out, sources, columns, offset, dirs):
        at = 0
        for x in sources:
            out[at : at + 21] = force[pl.ds(x, 21, stride=SX), :]
            at += 24
        for x in columns:
            out[at : at + 4] = below[pl.ds(FORCE_ROWS + x, 4, stride=WX), :]
            for y in range(4):
                out[at + 4 + y * 4 : at + 8 + y * 4] = moment[pl.ds(x * 4 + y, 4, stride=CELLS), :]
            out[at + 20 : at + 24] = above[pl.ds(FORCE_ROWS + x, 4, stride=WX), :]
            out[at + 24 : at + 28] = above[pl.ds(FORCE_ROWS + 4 * WX + x, 4, stride=WX), :]
            at += 32
        x = columns[0]
        for k, q in enumerate(dirs):
            row = offset + k * 4
            step = lattice_speeds[q][1]
            if step == 0:
                out[at : at + 4] = edge[row : row + 4]
            elif step == 1:
                source = FORCE_ROWS + 4 * WX + UP_Y.index(q) * WX + x
                out[at : at + 1] = below[source : source + 1]
                out[at + 1 : at + 4] = edge[row : row + 3]
            else:
                source = FORCE_ROWS + 8 * WX + DOWN_Y.index(q) * WX + x
                out[at : at + 3] = edge[row + 1 : row + 4]
                out[at + 3 : at + 4] = above[source : source + 1]
            at += 4

    outgoing(right, (15, 16, 17), (15,), 0, UP_X)
    outgoing(left, (23, 0, 1), (0, 1), 24, DOWN_X)


def collide_kernel(
    pop, force_in, moment, below, above, west, east, plane, z_high, z_low, fresh, sampled, force, ext, speed
):
    force[...] = force_in[...]
    for n, x in enumerate((23, 0, 1)):
        rows = pl.ds(x, 21, stride=SX)
        force[rows, :] = force[rows, :] + west[24 * n : 24 * n + 21]
    for n, x in enumerate((15, 16, 17)):
        rows = pl.ds(x, 21, stride=SX)
        force[rows, :] = force[rows, :] + east[24 * n : 24 * n + 21]

    for slab in range(SY):
        for q in range(4):
            row = (slab * 4 + q) * SX
            if slab == 0:
                value = below[FORCE_ROWS + q * WX : FORCE_ROWS + (q + 1) * WX]
            elif slab < 5:
                value = moment[pl.ds(q * CELLS + slab - 1, WX, stride=WY), :]
            else:
                source = FORCE_ROWS + ((slab - 5) * 4 + q) * WX
                value = above[source : source + WX]
            ext[row : row + WX] = value
            ext[row + WX : row + SX] = jnp.ones((8, NZ), f32)
    ext[pl.ds(23, 28, stride=SX), :] = west[72 : 72 + 28]
    ext[pl.ds(16, 28, stride=SX), :] = east[72 : 72 + 28]
    ext[pl.ds(17, 28, stride=SX), :] = east[104 : 104 + 28]

    rate = 1.0 / relax_time
    gain = 1.0 - 0.5 / relax_time
    for slab in range(SY):
        density = ext[slab * 4 * SX : (slab * 4 + 1) * SX]
        inverse = 1.0 / density
        pull = [force[(slab * 3 + c) * SX : (slab * 3 + c + 1) * SX] for c in range(3)]
        flow = [
            (ext[(slab * 4 + 1 + c) * SX : (slab * 4 + 2 + c) * SX] + 0.5 * pull[c]) * inverse
            for c in range(3)
        ]
        for c in range(3):
            high, low = halves(flow[c])
            row = (c * SY + slab) * SX
            speed[row : row + SX, 0:NZ] = high.astype(f32)
            speed[row : row + SX, NZ : 2 * NZ] = low.astype(f32)
        if slab == SY - 1:
            continue
        y_from = slab - 1
        square = flow[0] * flow[0] + flow[1] * flow[1] + flow[2] * flow[2]
        work = flow[0] * pull[0] + flow[1] * pull[1] + flow[2] * pull[2]
        scaled = rate * density
        constant = scaled * (1.0 - 1.5 * square) - (3.0 * gain) * work
        linear = 3.0 * scaled
        quadratic = 4.5 * scaled
        for q in range(19):
            step_x, step_y, step_z = lattice_speeds[q]
            y_to = y_from + step_y
            if y_to < 0 or y_to > 3:
                continue
            if 0 <= y_from <= 3:
                value = pop[pl.ds(q * CELLS + y_from, WX, stride=WY), :]
            elif y_from < 0:
                source = FORCE_ROWS + 4 * WX + UP_Y.index(q) * WX
                value = below[source : source + WX]
            else:
                source = FORCE_ROWS + 8 * WX + DOWN_Y.index(q) * WX
                value = above[source : source + WX]
            if step_x == 1:
                row = 104 + UP_X.index(q) * 4 + y_to
                value = jnp.concatenate(
                    [value, jnp.broadcast_to(west[row : row + 1], (8, NZ))], axis=0
                )
            elif step_x == -1:
                row = 136 + DOWN_X.index(q) * 4 + y_to
                value = jnp.concatenate(
                    [value, jnp.broadcast_to(east[row : row + 1], (8, NZ))], axis=0
                )
            extent = value.shape[0]

            def directed(vectors):
                total = None
                for c in range(3):
                    s = lattice_speeds[q][c]
                    if s:
                        term = vectors[c][0:extent]
                        if total is None:
                            total = term if s > 0 else -term
                        else:
                            total = total + term if s > 0 else total - term
                return total

            balance = constant[0:extent]
            if q:
                cu = directed(flow)
                cf = directed(pull)
                balance = (
                    balance
                    + cu * (linear[0:extent] + quadratic[0:extent] * cu + (9.0 * gain) * cf)
                    + (3.0 * gain) * cf
                )
            post = (1.0 - rate) * value + lattice_weights[q] * balance
            if step_x:
                post = pltpu.roll(post, step_x % SX, 0)[0:WX]
            if step_z:
                post = pltpu.roll(post, step_z % NZ, 1)
            fresh[pl.ds(q * CELLS + y_to, WX, stride=WY), :] = post

    both = jnp.concatenate([z_high[...], z_high[...]], axis=0)
    rows = SY * SX
    for c in range(3):
        split = speed[c * rows : (c + 1) * rows].astype(bf16)
        value = jnp.dot(split, both, preferred_element_type=f32) + jnp.dot(
            split[:, 0:NZ], z_low[...], preferred_element_type=f32
        )
        sampled[c : c + 1] = jnp.sum(value * plane[...], axis=0, keepdims=True)


def call(kernel, outputs, scratch, name, operands):
    vmem = pl.BlockSpec(memory_space=pltpu.VMEM)
    return pl.pallas_call(
        kernel,
        out_shape=[jax.ShapeDtypeStruct(shape, kind) for shape, kind in outputs],
        in_specs=[vmem] * len(operands),
        out_specs=[vmem] * len(outputs),
        scratch_shapes=[pltpu.VMEM(shape, f32) for shape in scratch],
        compiler_params=pltpu.CompilerParams(vmem_limit_bytes=32 * 1024 * 1024),
        name=name,
    )(*operands)


def shift(value, axis, step):
    size = lax.axis_size(axis)
    return lax.ppermute(value, axis, [(i, (i + step) % size) for i in range(size)])


def per_device(populations, vert_base, vert_frac, edges, stiffness, rest):
    pop = populations.reshape(19 * CELLS, NZ)
    force, moment, plane, z_high, z_low, edge, up, down = call(
        spread_kernel,
        [
            ((SY * 3 * SX, NZ), f32),
            ((4 * CELLS, NZ), f32),
            ((SY * SX, VERTS), f32),
            ((NZ, VERTS), bf16),
            ((NZ, VERTS), bf16),
            ((48, NZ), f32),
            ((UP_ROWS, NZ), f32),
            ((DOWN_ROWS, NZ), f32),
        ],
        [],
        "spread",
        [pop, vert_base, vert_frac, edges, stiffness.reshape(1, EDGES), rest],
    )
    below = shift(up, "gy", 1)
    above = shift(down, "gy", -1)
    force, right, left = call(
        merge_kernel,
        [((SY * 3 * SX, NZ), f32), ((RIGHT_ROWS, NZ), f32), ((LEFT_ROWS, NZ), f32)],
        [],
        "merge",
        [force, moment, edge, below, above],
    )
    west = shift(right, "gx", 1)
    east = shift(left, "gx", -1)
    fresh, sampled = call(
        collide_kernel,
        [((19 * CELLS, NZ), f32), ((3, VERTS), f32)],
        [(SY * 3 * SX, NZ), (SY * 4 * SX, NZ), (SY * 3 * SX, 2 * NZ)],
        "collide",
        [pop, force, moment, below, above, west, east, plane, z_high, z_low],
    )
    return fresh.reshape(19, WX, WY, NZ), sampled


def solution(mesh):
    placed = (
        P(None, "gx", "gy", None),
        P(None, ("gx", "gy")),
        P(None, ("gx", "gy")),
        P(None, ("gx", "gy")),
        P(("gx", "gy")),
        P(None, ("gx", "gy")),
    )
    return jax.shard_map(
        per_device,
        mesh=mesh,
        in_specs=placed,
        out_specs=(P(None, "gx", "gy", None), P(None, ("gx", "gy"))),
        check_vma=False,
    )
```

```python
import jax
import jax.numpy as jnp
from jax import lax
from jax.experimental import pallas as pl
from jax.experimental.pallas import tpu as pltpu
from jax.sharding import PartitionSpec as P

lattice_speeds = [
    (0, 0, 0),
    (1, 0, 0),
    (-1, 0, 0),
    (0, 1, 0),
    (0, -1, 0),
    (0, 0, 1),
    (0, 0, -1),
    (1, 1, 0),
    (-1, -1, 0),
    (1, -1, 0),
    (-1, 1, 0),
    (1, 0, 1),
    (-1, 0, -1),
    (1, 0, -1),
    (-1, 0, 1),
    (0, 1, 1),
    (0, -1, -1),
    (0, 1, -1),
    (0, -1, 1),
]
lattice_weights = [1.0 / 3.0] + [1.0 / 18.0] * 6 + [1.0 / 36.0] * 12
relax_time = 0.9

f32 = jnp.float32
bf16 = jnp.bfloat16

WX, WY, NZ = 16, 4, 128
CELLS = WX * WY
VERTS, TILE, EDGES = 512, 128, 1536
SX, SY = 24, 7

UP_Y = [q for q in range(19) if lattice_speeds[q][1] == 1]
DOWN_Y = [q for q in range(19) if lattice_speeds[q][1] == -1]
UP_X = [q for q in range(19) if lattice_speeds[q][0] == 1]
DOWN_X = [q for q in range(19) if lattice_speeds[q][0] == -1]

FORCE_ROWS = 9 * WX + 32
POP_ROWS = FORCE_ROWS + 4 * WX
BEHIND_ROWS = POP_ROWS + 5 * WX
STRIP_ROWS = BEHIND_ROWS + WX
SIDE_ROWS = 3 * 24 + 2 * 32 + 24


def outer_weight(r):
    return (5.0 - 2.0 * r - jnp.sqrt(-7.0 + 12.0 * r - 4.0 * r * r)) / 8.0


def inner_weight(r):
    return (3.0 - 2.0 * r + jnp.sqrt(1.0 + 4.0 * r - 4.0 * r * r)) / 8.0


def halves(value):
    high = value.astype(bf16)
    low = (value - high.astype(f32)).astype(bf16)
    return high, low


def along_last(a, b):
    return lax.dot_general(a, b, (((1,), (1,)), ((), ())), preferred_element_type=f32)


def iota(shape, dim):
    return lax.broadcasted_iota(jnp.int32, shape, dim)


def edge_forces(base, frac, edges, stiffness, rest, row):
    head = edges[0:1]
    tail = edges[1:2]
    run = head >> 7
    local = jnp.concatenate([row] * (EDGES // NZ), axis=1)
    plus = local == (tail & (TILE - 1))
    minus = local == (head & (TILE - 1))
    signed = jnp.where(plus, 1.0, jnp.where(minus, -1.0, 0.0)).astype(bf16)
    whole = base.astype(f32)
    high, low = halves(frac)
    blank = jnp.zeros((5, TILE), f32)
    pieces = []
    for part in (whole, high.astype(f32), low.astype(f32)):
        for t in range(4):
            pieces += [part[:, t * TILE : (t + 1) * TILE], blank]
    stacked = jnp.concatenate(pieces, axis=0).astype(bf16)
    found = jnp.dot(stacked, signed, preferred_element_type=f32)
    found = found[0:32] + found[32:64] + found[64:96]
    apart = jnp.zeros((8, EDGES), f32)
    for t in range(4):
        apart = apart + jnp.where(run == t, found[8 * t : 8 * t + 8], 0.0)
    stretch = stiffness * (apart[0:3] - rest)
    high, low = halves(stretch)
    blank = jnp.zeros((5, EDGES), f32)
    pieces = []
    for part in (high.astype(f32), low.astype(f32)):
        for t in range(4):
            pieces += [jnp.where(run == t, part, 0.0), blank]
    stacked = jnp.concatenate(pieces, axis=0).astype(bf16)
    pulled = along_last(stacked, signed)
    pulled = pulled[0:32] + pulled[32:64]
    return jnp.concatenate([-pulled[8 * t : 8 * t + 3] for t in range(4)], axis=1)


def rows_kernel(row):
    row[...] = iota((TILE, NZ), 0)


def spread_kernel(
    pop,
    base,
    frac,
    edges,
    stiffness,
    rest,
    row,
    force,
    moment,
    plane_out,
    high_out,
    low_out,
    edge_out,
    even_strip,
    odd_strip,
):
    springs = jnp.concatenate([stiffness[k : k + 1] for k in range(EDGES // NZ)], axis=1)
    row = row[...]
    membrane = edge_forces(base[...], frac[...], edges[...], springs, rest[...], row)
    cell = base[...]
    part = frac[...]
    kernel = [
        outer_weight(1.0 + part),
        inner_weight(part),
        inner_weight(1.0 - part),
        outer_weight(2.0 - part),
    ]

    def columns(rows, offset, dim):
        total = jnp.zeros((rows, VERTS), f32)
        for step in range(4):
            total = jnp.where(offset == step, kernel[step][dim : dim + 1], total)
        return total

    slot = iota((SX, VERTS), 0)
    slot = jnp.where(slot == SX - 1, -1, slot)
    along_x = columns(SX, slot - (cell[0:1] & (WX - 1)) + 1, 0)
    slab = iota((8, VERTS), 0)
    along_y = columns(8, slab - (cell[1:2] & (WY - 1)), 1)
    depth = iota((NZ, VERTS), 0)
    along_z = columns(NZ, (depth - cell[2:3] + 1) & (NZ - 1), 2)
    plane = jnp.concatenate([along_x * along_y[y : y + 1] for y in range(SY)], axis=0)
    plane_out[...] = plane
    z_high, z_low = halves(along_z)
    high_out[...] = z_high
    low_out[...] = z_low

    plane_high, plane_low = halves(plane)
    for c in range(3):
        load_high, load_low = halves(along_z * membrane[c : c + 1])
        result = (
            along_last(plane_high, load_high)
            + along_last(plane_low, load_high)
            + along_last(plane_high, load_low)
        )
        for y in range(SY):
            force[(y * 3 + c) * SX : (y * 3 + c + 1) * SX] = result[y * SX : (y + 1) * SX]

    density = pop[0:CELLS]
    moments = [None, None, None]
    for q in range(1, 19):
        value = pop[q * CELLS : (q + 1) * CELLS]
        density = density + value
        for d in range(3):
            c = lattice_speeds[q][d]
            if c:
                if moments[d] is None:
                    moments[d] = value if c > 0 else -value
                else:
                    moments[d] = moments[d] + value if c > 0 else moments[d] - value
    moment[0:CELLS] = density
    for d in range(3):
        moment[(d + 1) * CELLS : (d + 2) * CELLS] = moments[d]

    def strip(out, slab, dirs, edge_row, behind):
        for k in range(9):
            value = force[(slab * 3 + k) * SX : (slab * 3 + k) * SX + WX]
            if behind is not None and k >= 6:
                source = (k - 5) * CELLS + behind
                value = value + 2.0 * moment[pl.ds(source, WX, stride=WY), :]
            out[k * WX : (k + 1) * WX] = value
        for n, x in enumerate((16, 17, 23)):
            at = 9 * WX + 9 * n
            out[at : at + 9] = force[pl.ds(slab * 3 * SX + x, 9, stride=SX), :]
        for q in range(4):
            at = FORCE_ROWS + q * WX
            out[at : at + WX] = moment[pl.ds(q * CELLS + edge_row, WX, stride=WY), :]
        for k, q in enumerate(dirs):
            at = POP_ROWS + k * WX
            out[at : at + WX] = pop[pl.ds(q * CELLS + edge_row, WX, stride=WY), :]
        if behind is not None:
            out[BEHIND_ROWS:STRIP_ROWS] = moment[pl.ds(behind, WX, stride=WY), :]

    odd = lax.axis_index("gy") & 1

    @pl.when(odd == 0)
    def _():
        strip(even_strip, 4, UP_Y, 3, None)
        strip(odd_strip, 0, DOWN_Y, 0, 1)

    @pl.when(odd == 1)
    def _():
        strip(odd_strip, 4, UP_Y, 3, None)
        strip(even_strip, 0, DOWN_Y, 0, 1)

    for k, q in enumerate(UP_X):
        edge_out[k * 4 : k * 4 + 4] = pop[q * CELLS + 60 : q * CELLS + 64]
    for k, q in enumerate(DOWN_X):
        edge_out[24 + k * 4 : 24 + k * 4 + 4] = pop[q * CELLS : q * CELLS + 4]


def merge_kernel(force_in, moment, edge, even_strip, odd_strip, force, right, left, below, above):
    odd = lax.axis_index("gy") & 1

    @pl.when(odd == 0)
    def _():
        below[...] = odd_strip[...]
        above[...] = even_strip[...]

    @pl.when(odd == 1)
    def _():
        below[...] = even_strip[...]
        above[...] = odd_strip[...]

    def outer(block, slab):
        for k in range(9):
            row = (slab * 3 + k) * SX
            force[row : row + WX] = force_in[row : row + WX] + block[k * WX : k * WX + WX]
        for n, x in enumerate((16, 17, 23)):
            rows = pl.ds(slab * 3 * SX + x, 9, stride=SX)
            at = 9 * WX + 9 * n
            force[rows, :] = force_in[rows, :] + block[at : at + 9]

    for k in range(9, 12):
        force[k * SX : (k + 1) * SX] = force_in[k * SX : (k + 1) * SX]
    for slab in (0, 4):
        for k in range(9):
            row = (slab * 3 + k) * SX + 16
            force[row : row + 8] = force_in[row : row + 8]
    outer(below, 0)
    outer(above, 4)

    def outgoing(out, sources, columns, offset, dirs):
        at = 0
        for x in sources:
            out[at : at + 21] = force[pl.ds(x, 21, stride=SX), :]
            at += 24
        for x in columns:
            out[at : at + 4] = below[pl.ds(FORCE_ROWS + x, 4, stride=WX), :]
            for y in range(4):
                out[at + 4 + y * 4 : at + 8 + y * 4] = moment[pl.ds(x * 4 + y, 4, stride=CELLS), :]
            out[at + 20 : at + 24] = above[pl.ds(FORCE_ROWS + x, 4, stride=WX), :]
            out[at + 24 : at + 25] = above[BEHIND_ROWS + x : BEHIND_ROWS + x + 1]
            out[at + 25 : at + 28] = jnp.zeros((3, NZ), f32)
            at += 32
        x = columns[0]
        for k, q in enumerate(dirs):
            row = offset + k * 4
            step = lattice_speeds[q][1]
            if step == 0:
                out[at : at + 4] = edge[row : row + 4]
            elif step == 1:
                source = POP_ROWS + UP_Y.index(q) * WX + x
                out[at : at + 1] = below[source : source + 1]
                out[at + 1 : at + 4] = edge[row : row + 3]
            else:
                source = POP_ROWS + DOWN_Y.index(q) * WX + x
                out[at : at + 3] = edge[row + 1 : row + 4]
                out[at + 3 : at + 4] = above[source : source + 1]
            at += 4

    outgoing(right, (15, 16, 17), (15,), 0, UP_X)
    outgoing(left, (23, 0, 1), (0, 1), 24, DOWN_X)


def collide_kernel(
    pop, force_in, moment, below, above, west, east, plane, z_high, z_low, fresh, sampled, force, ext, speed
):
    force[...] = force_in[...]
    for n, x in enumerate((23, 0, 1)):
        rows = pl.ds(x, 21, stride=SX)
        force[rows, :] = force[rows, :] + west[24 * n : 24 * n + 21]
    for n, x in enumerate((15, 16, 17)):
        rows = pl.ds(x, 21, stride=SX)
        force[rows, :] = force[rows, :] + east[24 * n : 24 * n + 21]

    for slab in range(SY):
        for q in range(4):
            row = (slab * 4 + q) * SX
            if slab == 0:
                value = below[FORCE_ROWS + q * WX : FORCE_ROWS + (q + 1) * WX]
            elif slab < 5:
                value = moment[pl.ds(q * CELLS + slab - 1, WX, stride=WY), :]
            elif slab == 5:
                value = above[FORCE_ROWS + q * WX : FORCE_ROWS + (q + 1) * WX]
            elif q == 0:
                value = above[BEHIND_ROWS:STRIP_ROWS]
            else:
                value = jnp.zeros((WX, NZ), f32)
            ext[row : row + WX] = value
            ext[row + WX : row + SX] = jnp.ones((8, NZ), f32)
    ext[pl.ds(23, 28, stride=SX), :] = west[72 : 72 + 28]
    ext[pl.ds(16, 28, stride=SX), :] = east[72 : 72 + 28]
    ext[pl.ds(17, 28, stride=SX), :] = east[104 : 104 + 28]

    rate = 1.0 / relax_time
    gain = 1.0 - 0.5 / relax_time
    for slab in range(SY):
        density = ext[slab * 4 * SX : (slab * 4 + 1) * SX]
        inverse = 1.0 / density
        pull = [force[(slab * 3 + c) * SX : (slab * 3 + c + 1) * SX] for c in range(3)]
        flow = [
            (ext[(slab * 4 + 1 + c) * SX : (slab * 4 + 2 + c) * SX] + 0.5 * pull[c]) * inverse
            for c in range(3)
        ]
        for c in range(3):
            high, low = halves(flow[c])
            row = (c * SY + slab) * SX
            speed[row : row + SX, 0:NZ] = high.astype(f32)
            speed[row : row + SX, NZ : 2 * NZ] = low.astype(f32)
        if slab == SY - 1:
            continue
        y_from = slab - 1
        square = flow[0] * flow[0] + flow[1] * flow[1] + flow[2] * flow[2]
        work = flow[0] * pull[0] + flow[1] * pull[1] + flow[2] * pull[2]
        scaled = rate * density
        constant = scaled * (1.0 - 1.5 * square) - (3.0 * gain) * work
        linear = 3.0 * scaled
        quadratic = 4.5 * scaled
        for q in range(19):
            step_x, step_y, step_z = lattice_speeds[q]
            y_to = y_from + step_y
            if y_to < 0 or y_to > 3:
                continue
            if 0 <= y_from <= 3:
                value = pop[pl.ds(q * CELLS + y_from, WX, stride=WY), :]
            elif y_from < 0:
                source = POP_ROWS + UP_Y.index(q) * WX
                value = below[source : source + WX]
            else:
                source = POP_ROWS + DOWN_Y.index(q) * WX
                value = above[source : source + WX]
            if step_x == 1:
                row = 104 + UP_X.index(q) * 4 + y_to
                value = jnp.concatenate(
                    [value, jnp.broadcast_to(west[row : row + 1], (8, NZ))], axis=0
                )
            elif step_x == -1:
                row = 136 + DOWN_X.index(q) * 4 + y_to
                value = jnp.concatenate(
                    [value, jnp.broadcast_to(east[row : row + 1], (8, NZ))], axis=0
                )
            extent = value.shape[0]

            def directed(vectors):
                total = None
                for c in range(3):
                    s = lattice_speeds[q][c]
                    if s:
                        term = vectors[c][0:extent]
                        if total is None:
                            total = term if s > 0 else -term
                        else:
                            total = total + term if s > 0 else total - term
                return total

            balance = constant[0:extent]
            if q:
                cu = directed(flow)
                cf = directed(pull)
                balance = (
                    balance
                    + cu * (linear[0:extent] + quadratic[0:extent] * cu + (9.0 * gain) * cf)
                    + (3.0 * gain) * cf
                )
            post = (1.0 - rate) * value + lattice_weights[q] * balance
            if step_x:
                post = pltpu.roll(post, step_x % SX, 0)[0:WX]
            if step_z:
                post = pltpu.roll(post, step_z % NZ, 1)
            fresh[pl.ds(q * CELLS + y_to, WX, stride=WY), :] = post

    both = jnp.concatenate([z_high[...], z_high[...]], axis=0)
    rows = SY * SX
    for c in range(3):
        split = speed[c * rows : (c + 1) * rows].astype(bf16)
        value = jnp.dot(split, both, preferred_element_type=f32) + jnp.dot(
            split[:, 0:NZ], z_low[...], preferred_element_type=f32
        )
        sampled[c : c + 1] = jnp.sum(value * plane[...], axis=0, keepdims=True)


def call(kernel, outputs, scratch, name, operands, cost=None):
    return pl.pallas_call(
        kernel,
        out_shape=[jax.ShapeDtypeStruct(shape, kind) for shape, kind in outputs],
        in_specs=[pl.BlockSpec(memory_space=pltpu.VMEM)] * len(operands),
        out_specs=[pl.BlockSpec(memory_space=pltpu.VMEM)] * len(outputs),
        scratch_shapes=scratch,
        compiler_params=pltpu.CompilerParams(vmem_limit_bytes=32 * 1024 * 1024),
        name=name,
        cost_estimate=cost,
    )(*operands)


def shift(value, axis, step):
    size = lax.axis_size(axis)
    return lax.ppermute(value, axis, [(i, (i + step) % size) for i in range(size)])


def swap(value, axis, first):
    size = lax.axis_size(axis)
    pairs = []
    for i in range(first, size + first, 2):
        pairs += [(i % size, (i + 1) % size), ((i + 1) % size, i % size)]
    return lax.ppermute(value, axis, pairs)


def per_device(populations, vert_base, vert_frac, edges, stiffness, rest):
    pop = populations.reshape(19 * CELLS, NZ)
    cost = pl.CostEstimate(flops=1 << 30, bytes_accessed=1 << 23, transcendentals=0)
    (row,) = call(rows_kernel, [((TILE, NZ), jnp.int32)], [], "rows", [], cost)
    force, moment, plane, z_high, z_low, edge, even_strip, odd_strip = call(
        spread_kernel,
        [
            ((SY * 3 * SX, NZ), f32),
            ((4 * CELLS, NZ), f32),
            ((SY * SX, VERTS), f32),
            ((NZ, VERTS), bf16),
            ((NZ, VERTS), bf16),
            ((48, NZ), f32),
            ((STRIP_ROWS, NZ), f32),
            ((STRIP_ROWS, NZ), f32),
        ],
        [],
        "spread",
        [pop, vert_base, vert_frac, edges, stiffness.reshape(EDGES // NZ, NZ), rest, row],
    )
    even_strip = swap(even_strip, "gy", 0)
    odd_strip = swap(odd_strip, "gy", 1)
    force, right, left, below, above = call(
        merge_kernel,
        [
            ((SY * 3 * SX, NZ), f32),
            ((SIDE_ROWS, NZ), f32),
            ((SIDE_ROWS, NZ), f32),
            ((STRIP_ROWS, NZ), f32),
            ((STRIP_ROWS, NZ), f32),
        ],
        [],
        "merge",
        [force, moment, edge, even_strip, odd_strip],
    )
    west = shift(right, "gx", 1)
    east = shift(left, "gx", -1)
    fresh, sampled = call(
        collide_kernel,
        [((19 * CELLS, NZ), f32), ((3, VERTS), f32)],
        [
            pltpu.VMEM((SY * 3 * SX, NZ), f32),
            pltpu.VMEM((SY * 4 * SX, NZ), f32),
            pltpu.VMEM((SY * 3 * SX, 2 * NZ), f32),
        ],
        "collide",
        [pop, force, moment, below, above, west, east, plane, z_high, z_low],
    )
    return fresh.reshape(19, WX, WY, NZ), sampled


def solution(mesh):
    placed = (
        P(None, "gx", "gy", None),
        P(None, ("gx", "gy")),
        P(None, ("gx", "gy")),
        P(None, ("gx", "gy")),
        P(("gx", "gy")),
        P(None, ("gx", "gy")),
    )
    return jax.shard_map(
        per_device,
        mesh=mesh,
        in_specs=placed,
        out_specs=(P(None, "gx", "gy", None), P(None, ("gx", "gy"))),
        check_vma=False,
    )
```

```python
import jax
import jax.numpy as jnp
from jax import lax
from jax.experimental import pallas as pl
from jax.experimental.pallas import tpu as pltpu
from jax.sharding import PartitionSpec as P

lattice_speeds = [
    (0, 0, 0),
    (1, 0, 0),
    (-1, 0, 0),
    (0, 1, 0),
    (0, -1, 0),
    (0, 0, 1),
    (0, 0, -1),
    (1, 1, 0),
    (-1, -1, 0),
    (1, -1, 0),
    (-1, 1, 0),
    (1, 0, 1),
    (-1, 0, -1),
    (1, 0, -1),
    (-1, 0, 1),
    (0, 1, 1),
    (0, -1, -1),
    (0, 1, -1),
    (0, -1, 1),
]
lattice_weights = [1.0 / 3.0] + [1.0 / 18.0] * 6 + [1.0 / 36.0] * 12
relax_time = 0.9

f32 = jnp.float32
bf16 = jnp.bfloat16

WX, WY, NZ = 16, 4, 128
CELLS = WX * WY
VERTS, TILE, EDGES = 512, 128, 1536
SX, SY = 24, 7

UP_Y = [q for q in range(19) if lattice_speeds[q][1] == 1]
DOWN_Y = [q for q in range(19) if lattice_speeds[q][1] == -1]
UP_X = [q for q in range(19) if lattice_speeds[q][0] == 1]
DOWN_X = [q for q in range(19) if lattice_speeds[q][0] == -1]

FORCE_ROWS = 64
MARK_ROW = 57
POP_ROWS = FORCE_ROWS + 4 * WX
UP_ROWS = POP_ROWS + 5 * WX
STRIP_ROWS = UP_ROWS + 4 * WX
SIDE_ROWS = 3 * 24 + 2 * 32 + 24


def outer_weight(r):
    return (5.0 - 2.0 * r - jnp.sqrt(-7.0 + 12.0 * r - 4.0 * r * r)) / 8.0


def inner_weight(r):
    return (3.0 - 2.0 * r + jnp.sqrt(1.0 + 4.0 * r - 4.0 * r * r)) / 8.0


def halves(value):
    high = value.astype(bf16)
    low = (value - high.astype(f32)).astype(bf16)
    return high, low


def along_last(a, b):
    return lax.dot_general(a, b, (((1,), (1,)), ((), ())), preferred_element_type=f32)


def iota(shape, dim):
    return lax.broadcasted_iota(jnp.int32, shape, dim)


def edge_forces(base, frac, edges, stiffness, rest, row):
    head = edges[0:1]
    tail = edges[1:2]
    run = head >> 7
    local = jnp.concatenate([row] * (EDGES // NZ), axis=1)
    plus = local == (tail & (TILE - 1))
    minus = local == (head & (TILE - 1))
    signed = jnp.where(plus, 1.0, jnp.where(minus, -1.0, 0.0)).astype(bf16)
    whole = base.astype(f32)
    high, low = halves(frac)
    blank = jnp.zeros((5, TILE), f32)
    pieces = []
    for part in (whole, high.astype(f32), low.astype(f32)):
        for t in range(4):
            pieces += [part[:, t * TILE : (t + 1) * TILE], blank]
    stacked = jnp.concatenate(pieces, axis=0).astype(bf16)
    found = jnp.dot(stacked, signed, preferred_element_type=f32)
    found = found[0:32] + found[32:64] + found[64:96]
    apart = jnp.zeros((8, EDGES), f32)
    for t in range(4):
        apart = apart + jnp.where(run == t, found[8 * t : 8 * t + 8], 0.0)
    stretch = stiffness * (apart[0:3] - rest)
    high, low = halves(stretch)
    blank = jnp.zeros((5, EDGES), f32)
    pieces = []
    for part in (high.astype(f32), low.astype(f32)):
        for t in range(4):
            pieces += [jnp.where(run == t, part, 0.0), blank]
    stacked = jnp.concatenate(pieces, axis=0).astype(bf16)
    pulled = along_last(stacked, signed)
    pulled = pulled[0:32] + pulled[32:64]
    return jnp.concatenate([-pulled[8 * t : 8 * t + 3] for t in range(4)], axis=1)


def rows_kernel(row):
    row[...] = iota((TILE, NZ), 0)


def kernel_of(frac):
    return [
        outer_weight(1.0 + frac),
        inner_weight(frac),
        inner_weight(1.0 - frac),
        outer_weight(2.0 - frac),
    ]


def columns(kernel, offset):
    total = jnp.where(offset == 0, kernel[0], 0.0)
    for step in range(1, 4):
        total = jnp.where(offset == step, kernel[step], total)
    return total


def windows(lanes, marks):
    component = (iota((1, TILE), 1) >> 3) & 3
    depth = iota((NZ, TILE), 0).astype(f32)
    match = jnp.where(depth == marks, 1.0, 0.0)
    spots = jnp.concatenate([jnp.where(component == c, match, 0.0) for c in range(3)], axis=0)
    high, low = halves(lanes)
    rows = lanes.shape[0]
    both = jnp.concatenate([high.astype(f32), low.astype(f32)], axis=0).astype(bf16)
    wide = along_last(both, spots.astype(bf16))
    return wide[0:rows] + wide[rows : 2 * rows]


def strip(out, lanes, marks, moment, pop, slab, dirs, edge_row):
    for k in range(3):
        out[k * WX : (k + 1) * WX] = lanes[(slab + k) * SX : (slab + k) * SX + WX]
    for n, x in enumerate((16, 17, 23)):
        out[48 + 3 * n : 51 + 3 * n] = lanes[pl.ds(slab * SX + x, 3, stride=SX), :]
    out[MARK_ROW:FORCE_ROWS] = jnp.broadcast_to(marks[0:1], (FORCE_ROWS - MARK_ROW, NZ))
    for q in range(4):
        at = FORCE_ROWS + q * WX
        out[at : at + WX] = moment[pl.ds(q * CELLS + edge_row, WX, stride=WY), :]
    for k, q in enumerate(dirs):
        at = POP_ROWS + k * WX
        out[at : at + WX] = pop[pl.ds(q * CELLS + edge_row, WX, stride=WY), :]


def spread_kernel(
    pop,
    base,
    frac,
    edges,
    stiffness,
    rest,
    row,
    lanes,
    marks,
    plane_out,
    moment,
    edge_out,
    up,
    down,
):
    springs = jnp.concatenate([stiffness[k : k + 1] for k in range(EDGES // NZ)], axis=1)
    membrane = edge_forces(base[...], frac[...], edges[...], springs, rest[...], row[...])
    part = frac[...]
    kernel = kernel_of(part)
    cell = base[...]

    slot = iota((SX, VERTS), 0)
    slot = jnp.where(slot == SX - 1, -1, slot)
    along_x = columns([k[0:1] for k in kernel], slot - (cell[0:1] & (WX - 1)) + 1)
    slab = iota((8, VERTS), 0)
    along_y = columns([k[1:2] for k in kernel], slab - (cell[1:2] & (WY - 1)))
    plane = jnp.concatenate([along_x * along_y[y : y + 1] for y in range(SY)], axis=0)
    plane_out[...] = plane

    layer = iota((8, TILE), 0)
    lane = iota((1, TILE), 1)
    mark = jnp.zeros((1, TILE), jnp.int32)
    blocks = []
    for t in range(4):
        span = slice(t * TILE, (t + 1) * TILE)
        z = cell[2:3, span]
        apart = ((z - z[:, 0:1] + 64) & (NZ - 1)) - 64
        lowest = jnp.min(apart.astype(f32), axis=1, keepdims=True).astype(jnp.int32)
        along_z = columns([k[2:3, span] for k in kernel], layer - apart + lowest)
        start = z[:, 0:1] + lowest - 1
        mark = jnp.where(lane >> 5 == t, (start + (lane & 7)) & (NZ - 1), mark)
        block = [along_z * membrane[c : c + 1, span] for c in range(3)] + [jnp.zeros((8, TILE), f32)]
        row_of = [jnp.zeros((32, TILE), f32)] * 4
        row_of[t] = jnp.concatenate(block, axis=0)
        blocks.append(jnp.concatenate(row_of, axis=1))
    loaded = jnp.concatenate(blocks, axis=0)
    marks[...] = jnp.broadcast_to(mark.astype(f32), (8, TILE))
    plane_high, plane_low = halves(plane)
    load_high, load_low = halves(loaded)
    lanes[...] = (
        along_last(plane_high, load_high)
        + along_last(plane_low, load_high)
        + along_last(plane_high, load_low)
    )

    density = pop[0:CELLS]
    moments = [None, None, None]
    for q in range(1, 19):
        value = pop[q * CELLS : (q + 1) * CELLS]
        density = density + value
        for d in range(3):
            c = lattice_speeds[q][d]
            if c:
                if moments[d] is None:
                    moments[d] = value if c > 0 else -value
                else:
                    moments[d] = moments[d] + value if c > 0 else moments[d] - value
    moment[0:CELLS] = density
    for d in range(3):
        moment[(d + 1) * CELLS : (d + 2) * CELLS] = moments[d]
    strip(up, lanes, marks, moment, pop, 4, UP_Y, 3)
    strip(down, lanes, marks, moment, pop, 0, DOWN_Y, 0)
    for q in range(4):
        at = UP_ROWS + q * WX
        down[at : at + WX] = moment[pl.ds(q * CELLS + 1, WX, stride=WY), :]
    for k, q in enumerate(UP_X):
        edge_out[k * 4 : k * 4 + 4] = pop[q * CELLS + 60 : q * CELLS + 64]
    for k, q in enumerate(DOWN_X):
        edge_out[24 + k * 4 : 24 + k * 4 + 4] = pop[q * CELLS : q * CELLS + 4]


def tables_kernel(base, frac, lanes, marks, force, high_out, low_out):
    wide = windows(lanes[...], marks[0:1])
    for slab in range(SY):
        for c in range(3):
            row = (slab * 3 + c) * SX
            force[row : row + SX] = wide[slab * SX : (slab + 1) * SX, c * NZ : (c + 1) * NZ]
    kernel = kernel_of(frac[2:3])
    depth = iota((NZ, VERTS), 0)
    along_z = columns(kernel, (depth - base[2:3] + 1) & (NZ - 1))
    z_high, z_low = halves(along_z)
    high_out[...] = z_high
    low_out[...] = z_low


def outgoing(out, force, moment, edge, below, above, sources, spots, offset, dirs):
    at = 0
    for x in sources:
        out[at : at + 21] = force[pl.ds(x, 21, stride=SX), :]
        at += 24
    for x in spots:
        out[at : at + 4] = below[pl.ds(FORCE_ROWS + x, 4, stride=WX), :]
        for y in range(4):
            out[at + 4 + y * 4 : at + 8 + y * 4] = moment[pl.ds(x * 4 + y, 4, stride=CELLS), :]
        out[at + 20 : at + 24] = above[pl.ds(FORCE_ROWS + x, 4, stride=WX), :]
        out[at + 24 : at + 28] = above[pl.ds(UP_ROWS + x, 4, stride=WX), :]
        at += 32
    x = spots[0]
    for k, q in enumerate(dirs):
        row = offset + k * 4
        step = lattice_speeds[q][1]
        if step == 0:
            out[at : at + 4] = edge[row : row + 4]
        elif step == 1:
            source = POP_ROWS + UP_Y.index(q) * WX + x
            out[at : at + 1] = below[source : source + 1]
            out[at + 1 : at + 4] = edge[row : row + 3]
        else:
            source = POP_ROWS + DOWN_Y.index(q) * WX + x
            out[at : at + 3] = edge[row + 1 : row + 4]
            out[at + 3 : at + 4] = above[source : source + 1]
        at += 4


def merge_kernel(force_in, moment, edge, below, above, force, right, left):
    for row in range(0, SY * 3 * SX, SX):
        force[row : row + SX] = force_in[row : row + SX]
    for block, slab in ((below, 0), (above, 4)):
        wide = windows(block[0:FORCE_ROWS], block[MARK_ROW : MARK_ROW + 1])
        for c in range(3):
            part = wide[:, c * NZ : (c + 1) * NZ]
            for k in range(3):
                row = ((slab + k) * 3 + c) * SX
                force[row : row + WX] = force[row : row + WX] + part[k * WX : (k + 1) * WX]
            for n, x in enumerate((16, 17, 23)):
                rows = pl.ds((slab * 3 + c) * SX + x, 3, stride=3 * SX)
                force[rows, :] = force[rows, :] + part[48 + 3 * n : 51 + 3 * n]
    outgoing(right, force, moment, edge, below, above, (15, 16, 17), (15,), 0, UP_X)
    outgoing(left, force, moment, edge, below, above, (23, 0, 1), (0, 1), 24, DOWN_X)


def collide_kernel(
    pop, force_in, moment, below, above, west, east, plane, z_high, z_low, fresh, sampled, force, ext, speed
):
    force[...] = force_in[...]
    for n, x in enumerate((23, 0, 1)):
        rows = pl.ds(x, 21, stride=SX)
        force[rows, :] = force[rows, :] + west[24 * n : 24 * n + 21]
    for n, x in enumerate((15, 16, 17)):
        rows = pl.ds(x, 21, stride=SX)
        force[rows, :] = force[rows, :] + east[24 * n : 24 * n + 21]

    for slab in range(SY):
        for q in range(4):
            row = (slab * 4 + q) * SX
            if slab == 0:
                value = below[FORCE_ROWS + q * WX : FORCE_ROWS + (q + 1) * WX]
            elif slab < 5:
                value = moment[pl.ds(q * CELLS + slab - 1, WX, stride=WY), :]
            elif slab == 5:
                value = above[FORCE_ROWS + q * WX : FORCE_ROWS + (q + 1) * WX]
            else:
                value = above[UP_ROWS + q * WX : UP_ROWS + (q + 1) * WX]
            ext[row : row + WX] = value
            ext[row + WX : row + SX] = jnp.ones((8, NZ), f32)
    ext[pl.ds(23, 28, stride=SX), :] = west[72 : 72 + 28]
    ext[pl.ds(16, 28, stride=SX), :] = east[72 : 72 + 28]
    ext[pl.ds(17, 28, stride=SX), :] = east[104 : 104 + 28]

    rate = 1.0 / relax_time
    gain = 1.0 - 0.5 / relax_time
    for slab in range(SY):
        density = ext[slab * 4 * SX : (slab * 4 + 1) * SX]
        inverse = 1.0 / density
        pull = [force[(slab * 3 + c) * SX : (slab * 3 + c + 1) * SX] for c in range(3)]
        flow = [
            (ext[(slab * 4 + 1 + c) * SX : (slab * 4 + 2 + c) * SX] + 0.5 * pull[c]) * inverse
            for c in range(3)
        ]
        for c in range(3):
            high, low = halves(flow[c])
            row = (c * SY + slab) * SX
            speed[row : row + SX, 0:NZ] = high.astype(f32)
            speed[row : row + SX, NZ : 2 * NZ] = low.astype(f32)
        if slab == SY - 1:
            continue
        y_from = slab - 1
        square = flow[0] * flow[0] + flow[1] * flow[1] + flow[2] * flow[2]
        work = flow[0] * pull[0] + flow[1] * pull[1] + flow[2] * pull[2]
        scaled = rate * density
        constant = scaled * (1.0 - 1.5 * square) - (3.0 * gain) * work
        linear = 3.0 * scaled
        quadratic = 4.5 * scaled
        for q in range(19):
            step_x, step_y, step_z = lattice_speeds[q]
            y_to = y_from + step_y
            if y_to < 0 or y_to > 3:
                continue
            if 0 <= y_from <= 3:
                value = pop[pl.ds(q * CELLS + y_from, WX, stride=WY), :]
            elif y_from < 0:
                source = POP_ROWS + UP_Y.index(q) * WX
                value = below[source : source + WX]
            else:
                source = POP_ROWS + DOWN_Y.index(q) * WX
                value = above[source : source + WX]
            if step_x == 1:
                row = 104 + UP_X.index(q) * 4 + y_to
                value = jnp.concatenate(
                    [value, jnp.broadcast_to(west[row : row + 1], (8, NZ))], axis=0
                )
            elif step_x == -1:
                row = 136 + DOWN_X.index(q) * 4 + y_to
                value = jnp.concatenate(
                    [value, jnp.broadcast_to(east[row : row + 1], (8, NZ))], axis=0
                )
            extent = value.shape[0]

            def directed(vectors):
                total = None
                for c in range(3):
                    s = lattice_speeds[q][c]
                    if s:
                        term = vectors[c][0:extent]
                        if total is None:
                            total = term if s > 0 else -term
                        else:
                            total = total + term if s > 0 else total - term
                return total

            balance = constant[0:extent]
            if q:
                cu = directed(flow)
                cf = directed(pull)
                balance = (
                    balance
                    + cu * (linear[0:extent] + quadratic[0:extent] * cu + (9.0 * gain) * cf)
                    + (3.0 * gain) * cf
                )
            post = (1.0 - rate) * value + lattice_weights[q] * balance
            if step_x:
                post = pltpu.roll(post, step_x % SX, 0)[0:WX]
            if step_z:
                post = pltpu.roll(post, step_z % NZ, 1)
            fresh[pl.ds(q * CELLS + y_to, WX, stride=WY), :] = post

    both = jnp.concatenate([z_high[...], z_high[...]], axis=0)
    rows = SY * SX
    for c in range(3):
        split = speed[c * rows : (c + 1) * rows].astype(bf16)
        value = jnp.dot(split, both, preferred_element_type=f32) + jnp.dot(
            split[:, 0:NZ], z_low[...], preferred_element_type=f32
        )
        sampled[c : c + 1] = jnp.sum(value * plane[...], axis=0, keepdims=True)


def call(kernel, outputs, scratch, name, operands, cost=None):
    return pl.pallas_call(
        kernel,
        out_shape=[jax.ShapeDtypeStruct(shape, kind) for shape, kind in outputs],
        in_specs=[pl.BlockSpec(memory_space=pltpu.VMEM)] * len(operands),
        out_specs=[pl.BlockSpec(memory_space=pltpu.VMEM)] * len(outputs),
        scratch_shapes=scratch,
        compiler_params=pltpu.CompilerParams(vmem_limit_bytes=32 * 1024 * 1024),
        name=name,
        cost_estimate=cost,
    )(*operands)


def shift(value, axis, step):
    size = lax.axis_size(axis)
    return lax.ppermute(value, axis, [(i, (i + step) % size) for i in range(size)])


def per_device(populations, vert_base, vert_frac, edges, stiffness, rest):
    pop = populations.reshape(19 * CELLS, NZ)
    cost = pl.CostEstimate(flops=1 << 30, bytes_accessed=1 << 23, transcendentals=0)
    (row,) = call(rows_kernel, [((TILE, NZ), jnp.int32)], [], "rows", [], cost)
    lanes, marks, plane, moment, edge, up, down = call(
        spread_kernel,
        [
            ((SY * SX, NZ), f32),
            ((8, NZ), f32),
            ((SY * SX, VERTS), f32),
            ((4 * CELLS, NZ), f32),
            ((48, NZ), f32),
            ((STRIP_ROWS, NZ), f32),
            ((STRIP_ROWS, NZ), f32),
        ],
        [],
        "spread",
        [pop, vert_base, vert_frac, edges, stiffness.reshape(EDGES // NZ, NZ), rest, row],
    )
    below = shift(up, "gy", 1)
    above = shift(down, "gy", -1)
    force, z_high, z_low = call(
        tables_kernel,
        [((SY * 3 * SX, NZ), f32), ((NZ, VERTS), bf16), ((NZ, VERTS), bf16)],
        [],
        "tables",
        [vert_base, vert_frac, lanes, marks],
        cost,
    )
    force, right, left = call(
        merge_kernel,
        [((SY * 3 * SX, NZ), f32), ((SIDE_ROWS, NZ), f32), ((SIDE_ROWS, NZ), f32)],
        [],
        "merge",
        [force, moment, edge, below, above],
    )
    west = shift(right, "gx", 1)
    east = shift(left, "gx", -1)
    fresh, sampled = call(
        collide_kernel,
        [((19 * CELLS, NZ), f32), ((3, VERTS), f32)],
        [
            pltpu.VMEM((SY * 3 * SX, NZ), f32),
            pltpu.VMEM((SY * 4 * SX, NZ), f32),
            pltpu.VMEM((SY * 3 * SX, 2 * NZ), f32),
        ],
        "collide",
        [pop, force, moment, below, above, west, east, plane, z_high, z_low],
    )
    return fresh.reshape(19, WX, WY, NZ), sampled


def solution(mesh):
    placed = (
        P(None, "gx", "gy", None),
        P(None, ("gx", "gy")),
        P(None, ("gx", "gy")),
        P(None, ("gx", "gy")),
        P(("gx", "gy")),
        P(None, ("gx", "gy")),
    )
    return jax.shard_map(
        per_device,
        mesh=mesh,
        in_specs=placed,
        out_specs=(P(None, "gx", "gy", None), P(None, ("gx", "gy"))),
        check_vma=False,
    )
```

```python
import jax
import jax.numpy as jnp
from jax import lax
from jax.experimental import pallas as pl
from jax.experimental.pallas import tpu as pltpu
from jax.sharding import PartitionSpec as P

lattice_speeds = [
    (0, 0, 0),
    (1, 0, 0),
    (-1, 0, 0),
    (0, 1, 0),
    (0, -1, 0),
    (0, 0, 1),
    (0, 0, -1),
    (1, 1, 0),
    (-1, -1, 0),
    (1, -1, 0),
    (-1, 1, 0),
    (1, 0, 1),
    (-1, 0, -1),
    (1, 0, -1),
    (-1, 0, 1),
    (0, 1, 1),
    (0, -1, -1),
    (0, 1, -1),
    (0, -1, 1),
]
lattice_weights = [1.0 / 3.0] + [1.0 / 18.0] * 6 + [1.0 / 36.0] * 12
relax_time = 0.9

f32 = jnp.float32
bf16 = jnp.bfloat16

WX, WY, NZ = 16, 4, 128
CELLS = WX * WY
VERTS, TILE, EDGES = 512, 128, 1536
SX, SY = 24, 7

UP_Y = [q for q in range(19) if lattice_speeds[q][1] == 1]
DOWN_Y = [q for q in range(19) if lattice_speeds[q][1] == -1]
UP_X = [q for q in range(19) if lattice_speeds[q][0] == 1]
DOWN_X = [q for q in range(19) if lattice_speeds[q][0] == -1]

FORCE_ROWS = 64
MARK_ROW = 57
POP_ROWS = FORCE_ROWS + 4 * WX
UP_ROWS = POP_ROWS + 5 * WX
STRIP_ROWS = UP_ROWS + 4 * WX
SIDE_MOMENTS = 64
SIDE_DENSITY = 92
SIDE_POP = 100
SIDE_ROWS = 120


def outer_weight(r):
    return (5.0 - 2.0 * r - jnp.sqrt(-7.0 + 12.0 * r - 4.0 * r * r)) / 8.0


def inner_weight(r):
    return (3.0 - 2.0 * r + jnp.sqrt(1.0 + 4.0 * r - 4.0 * r * r)) / 8.0


def halves(value):
    high = value.astype(bf16)
    low = (value - high.astype(f32)).astype(bf16)
    return high, low


def along_last(a, b):
    return lax.dot_general(a, b, (((1,), (1,)), ((), ())), preferred_element_type=f32)


def iota(shape, dim):
    return lax.broadcasted_iota(jnp.int32, shape, dim)


def edge_forces(base, frac, edges, stiffness, rest, row):
    head = edges[0:1]
    tail = edges[1:2]
    run = head >> 7
    local = jnp.concatenate([row] * (EDGES // NZ), axis=1)
    plus = local == (tail & (TILE - 1))
    minus = local == (head & (TILE - 1))
    signed = jnp.where(plus, 1.0, jnp.where(minus, -1.0, 0.0)).astype(bf16)
    whole = base.astype(f32)
    high, low = halves(frac)
    blank = jnp.zeros((5, TILE), f32)
    pieces = []
    for part in (whole, high.astype(f32), low.astype(f32)):
        for t in range(4):
            pieces += [part[:, t * TILE : (t + 1) * TILE], blank]
    stacked = jnp.concatenate(pieces, axis=0).astype(bf16)
    found = jnp.dot(stacked, signed, preferred_element_type=f32)
    found = found[0:32] + found[32:64] + found[64:96]
    apart = jnp.zeros((8, EDGES), f32)
    for t in range(4):
        apart = apart + jnp.where(run == t, found[8 * t : 8 * t + 8], 0.0)
    stretch = stiffness * (apart[0:3] - rest)
    high, low = halves(stretch)
    blank = jnp.zeros((5, EDGES), f32)
    pieces = []
    for part in (high.astype(f32), low.astype(f32)):
        for t in range(4):
            pieces += [jnp.where(run == t, part, 0.0), blank]
    stacked = jnp.concatenate(pieces, axis=0).astype(bf16)
    pulled = along_last(stacked, signed)
    pulled = pulled[0:32] + pulled[32:64]
    return jnp.concatenate([-pulled[8 * t : 8 * t + 3] for t in range(4)], axis=1)


def rows_kernel(row):
    row[...] = iota((TILE, NZ), 0)


def kernel_of(frac):
    return [
        outer_weight(1.0 + frac),
        inner_weight(frac),
        inner_weight(1.0 - frac),
        outer_weight(2.0 - frac),
    ]


def columns(kernel, offset):
    total = jnp.where(offset == 0, kernel[0], 0.0)
    for step in range(1, 4):
        total = jnp.where(offset == step, kernel[step], total)
    return total


def windows(lanes, marks):
    component = (iota((1, TILE), 1) >> 3) & 3
    depth = iota((NZ, TILE), 0).astype(f32)
    match = jnp.where(depth == marks, 1.0, 0.0)
    spots = jnp.concatenate([jnp.where(component == c, match, 0.0) for c in range(3)], axis=0)
    high, low = halves(lanes)
    rows = lanes.shape[0]
    both = jnp.concatenate([high.astype(f32), low.astype(f32)], axis=0).astype(bf16)
    wide = along_last(both, spots.astype(bf16))
    return wide[0:rows] + wide[rows : 2 * rows]


def strip(out, lanes, marks, moment, pop, slab, dirs, edge_row):
    for k in range(3):
        out[k * WX : (k + 1) * WX] = lanes[(slab + k) * SX : (slab + k) * SX + WX]
    for n, x in enumerate((16, 17, 23)):
        out[48 + 3 * n : 51 + 3 * n] = lanes[pl.ds(slab * SX + x, 3, stride=SX), :]
    out[MARK_ROW:FORCE_ROWS] = jnp.broadcast_to(marks[0:1], (FORCE_ROWS - MARK_ROW, NZ))
    for q in range(4):
        at = FORCE_ROWS + q * WX
        out[at : at + WX] = moment[pl.ds(q * CELLS + edge_row, WX, stride=WY), :]
    for k, q in enumerate(dirs):
        at = POP_ROWS + k * WX
        out[at : at + WX] = pop[pl.ds(q * CELLS + edge_row, WX, stride=WY), :]


def spread_kernel(base, frac, edges, stiffness, rest, row, lanes, marks, plane_out):
    springs = jnp.concatenate([stiffness[k : k + 1] for k in range(EDGES // NZ)], axis=1)
    membrane = edge_forces(base[...], frac[...], edges[...], springs, rest[...], row[...])
    part = frac[...]
    kernel = kernel_of(part)
    cell = base[...]

    slot = iota((SX, VERTS), 0)
    slot = jnp.where(slot == SX - 1, -1, slot)
    along_x = columns([k[0:1] for k in kernel], slot - (cell[0:1] & (WX - 1)) + 1)
    slab = iota((8, VERTS), 0)
    along_y = columns([k[1:2] for k in kernel], slab - (cell[1:2] & (WY - 1)))
    plane = jnp.concatenate([along_x * along_y[y : y + 1] for y in range(SY)], axis=0)
    plane_out[...] = plane

    layer = iota((8, TILE), 0)
    lane = iota((1, TILE), 1)
    mark = jnp.zeros((1, TILE), jnp.int32)
    blocks = []
    for t in range(4):
        span = slice(t * TILE, (t + 1) * TILE)
        z = cell[2:3, span]
        apart = ((z - z[:, 0:1] + 64) & (NZ - 1)) - 64
        lowest = jnp.min(apart.astype(f32), axis=1, keepdims=True).astype(jnp.int32)
        along_z = columns([k[2:3, span] for k in kernel], layer - apart + lowest)
        start = z[:, 0:1] + lowest - 1
        mark = jnp.where(lane >> 5 == t, (start + (lane & 7)) & (NZ - 1), mark)
        block = [along_z * membrane[c : c + 1, span] for c in range(3)] + [jnp.zeros((8, TILE), f32)]
        row_of = [jnp.zeros((32, TILE), f32)] * 4
        row_of[t] = jnp.concatenate(block, axis=0)
        blocks.append(jnp.concatenate(row_of, axis=1))
    loaded = jnp.concatenate(blocks, axis=0)
    marks[...] = jnp.broadcast_to(mark.astype(f32), (8, TILE))
    plane_high, plane_low = halves(plane)
    load_high, load_low = halves(loaded)
    lanes[...] = (
        along_last(plane_high, load_high)
        + along_last(plane_low, load_high)
        + along_last(plane_high, load_low)
    )


def strips_kernel(pop, lanes, marks, moment, edge_out, up, down):
    density = pop[0:CELLS]
    moments = [None, None, None]
    for q in range(1, 19):
        value = pop[q * CELLS : (q + 1) * CELLS]
        density = density + value
        for d in range(3):
            c = lattice_speeds[q][d]
            if c:
                if moments[d] is None:
                    moments[d] = value if c > 0 else -value
                else:
                    moments[d] = moments[d] + value if c > 0 else moments[d] - value
    moment[0:CELLS] = density
    for d in range(3):
        moment[(d + 1) * CELLS : (d + 2) * CELLS] = moments[d]
    strip(up, lanes, marks, moment, pop, 4, UP_Y, 3)
    strip(down, lanes, marks, moment, pop, 0, DOWN_Y, 0)
    for q in range(4):
        at = UP_ROWS + q * WX
        down[at : at + WX] = moment[pl.ds(q * CELLS + 1, WX, stride=WY), :]
    for k, q in enumerate(UP_X):
        edge_out[k * 4 : k * 4 + 4] = pop[q * CELLS + 60 : q * CELLS + 64]
    for k, q in enumerate(DOWN_X):
        edge_out[24 + k * 4 : 24 + k * 4 + 4] = pop[q * CELLS : q * CELLS + 4]


def tables_kernel(base, frac, lanes, marks, force, high_out, low_out):
    wide = windows(lanes[...], marks[0:1])
    for slab in range(SY):
        for c in range(3):
            row = (slab * 3 + c) * SX
            force[row : row + SX] = wide[slab * SX : (slab + 1) * SX, c * NZ : (c + 1) * NZ]
    kernel = kernel_of(frac[2:3])
    depth = iota((NZ, VERTS), 0)
    along_z = columns(kernel, (depth - base[2:3] + 1) & (NZ - 1))
    z_high, z_low = halves(along_z)
    high_out[...] = z_high
    low_out[...] = z_low


def outgoing(out, force, moment, edge, below, above, sources, x, behind, offset, dirs):
    def moments_at(x, y, first):
        count = 4 - first
        if y < 0:
            return below[pl.ds(FORCE_ROWS + first * WX + x, count, stride=WX), :]
        if y < 4:
            return moment[pl.ds(first * CELLS + x * 4 + y, count, stride=CELLS), :]
        at = FORCE_ROWS if y == 4 else UP_ROWS
        return above[pl.ds(at + first * WX + x, count, stride=WX), :]

    for n, source in enumerate(sources):
        if source == behind:
            for y in range(SY):
                value = force[pl.ds(y * 3 * SX + source, 3, stride=SX), :]
                value = value + 2.0 * moments_at(source, y - 1, 1)
                out[21 * n + 3 * y : 21 * n + 3 * y + 3] = value
                out[SIDE_DENSITY + y : SIDE_DENSITY + y + 1] = moments_at(source, y - 1, 0)[0:1]
        else:
            out[21 * n : 21 * n + 21] = force[pl.ds(source, 21, stride=SX), :]
    for y in range(SY):
        out[SIDE_MOMENTS + 4 * y : SIDE_MOMENTS + 4 * y + 4] = moments_at(x, y - 1, 0)
    at = SIDE_POP
    for k, q in enumerate(dirs):
        row = offset + k * 4
        step = lattice_speeds[q][1]
        if step == 0:
            out[at : at + 4] = edge[row : row + 4]
        elif step == 1:
            source = POP_ROWS + UP_Y.index(q) * WX + x
            out[at : at + 1] = below[source : source + 1]
            out[at + 1 : at + 4] = edge[row : row + 3]
        else:
            source = POP_ROWS + DOWN_Y.index(q) * WX + x
            out[at : at + 3] = edge[row + 1 : row + 4]
            out[at + 3 : at + 4] = above[source : source + 1]
        at += 4


def merge_kernel(force_in, moment, edge, below, above, force, right, left):
    for row in range(0, SY * 3 * SX, SX):
        force[row : row + SX] = force_in[row : row + SX]
    for block, slab in ((below, 0), (above, 4)):
        wide = windows(block[0:FORCE_ROWS], block[MARK_ROW : MARK_ROW + 1])
        for c in range(3):
            part = wide[:, c * NZ : (c + 1) * NZ]
            for k in range(3):
                row = ((slab + k) * 3 + c) * SX
                force[row : row + WX] = force[row : row + WX] + part[k * WX : (k + 1) * WX]
            for n, x in enumerate((16, 17, 23)):
                rows = pl.ds((slab * 3 + c) * SX + x, 3, stride=3 * SX)
                force[rows, :] = force[rows, :] + part[48 + 3 * n : 51 + 3 * n]
    outgoing(right, force, moment, edge, below, above, (15, 16, 17), 15, None, 0, UP_X)
    outgoing(left, force, moment, edge, below, above, (23, 0, 1), 0, 1, 24, DOWN_X)


def collide_kernel(
    pop, force_in, moment, below, above, west, east, plane, z_high, z_low, fresh, sampled, force, ext, speed
):
    force[...] = force_in[...]
    for n, x in enumerate((23, 0, 1)):
        rows = pl.ds(x, 21, stride=SX)
        force[rows, :] = force[rows, :] + west[21 * n : 21 * n + 21]
    for n, x in enumerate((15, 16, 17)):
        rows = pl.ds(x, 21, stride=SX)
        force[rows, :] = force[rows, :] + east[21 * n : 21 * n + 21]

    for slab in range(SY):
        for q in range(4):
            row = (slab * 4 + q) * SX
            if slab == 0:
                value = below[FORCE_ROWS + q * WX : FORCE_ROWS + (q + 1) * WX]
            elif slab < 5:
                value = moment[pl.ds(q * CELLS + slab - 1, WX, stride=WY), :]
            elif slab == 5:
                value = above[FORCE_ROWS + q * WX : FORCE_ROWS + (q + 1) * WX]
            else:
                value = above[UP_ROWS + q * WX : UP_ROWS + (q + 1) * WX]
            ext[row : row + WX] = value
            ext[row + WX : row + SX] = jnp.full((8, NZ), 0.0 if q else 1.0, f32)
    ext[pl.ds(23, 28, stride=SX), :] = west[SIDE_MOMENTS : SIDE_MOMENTS + 28]
    ext[pl.ds(16, 28, stride=SX), :] = east[SIDE_MOMENTS : SIDE_MOMENTS + 28]
    ext[pl.ds(17, 7, stride=4 * SX), :] = east[SIDE_DENSITY : SIDE_DENSITY + 7]

    rate = 1.0 / relax_time
    gain = 1.0 - 0.5 / relax_time
    for slab in range(SY):
        density = ext[slab * 4 * SX : (slab * 4 + 1) * SX]
        inverse = 1.0 / density
        pull = [force[(slab * 3 + c) * SX : (slab * 3 + c + 1) * SX] for c in range(3)]
        flow = [
            (ext[(slab * 4 + 1 + c) * SX : (slab * 4 + 2 + c) * SX] + 0.5 * pull[c]) * inverse
            for c in range(3)
        ]
        for c in range(3):
            high, low = halves(flow[c])
            row = (c * SY + slab) * SX
            speed[row : row + SX, 0:NZ] = high.astype(f32)
            speed[row : row + SX, NZ : 2 * NZ] = low.astype(f32)
        if slab == SY - 1:
            continue
        y_from = slab - 1
        square = flow[0] * flow[0] + flow[1] * flow[1] + flow[2] * flow[2]
        work = flow[0] * pull[0] + flow[1] * pull[1] + flow[2] * pull[2]
        scaled = rate * density
        constant = scaled * (1.0 - 1.5 * square) - (3.0 * gain) * work
        linear = 3.0 * scaled
        quadratic = 4.5 * scaled
        for q in range(19):
            step_x, step_y, step_z = lattice_speeds[q]
            y_to = y_from + step_y
            if y_to < 0 or y_to > 3:
                continue
            if 0 <= y_from <= 3:
                value = pop[pl.ds(q * CELLS + y_from, WX, stride=WY), :]
            elif y_from < 0:
                source = POP_ROWS + UP_Y.index(q) * WX
                value = below[source : source + WX]
            else:
                source = POP_ROWS + DOWN_Y.index(q) * WX
                value = above[source : source + WX]
            if step_x == 1:
                row = SIDE_POP + UP_X.index(q) * 4 + y_to
                value = jnp.concatenate(
                    [value, jnp.broadcast_to(west[row : row + 1], (8, NZ))], axis=0
                )
            elif step_x == -1:
                row = SIDE_POP + DOWN_X.index(q) * 4 + y_to
                value = jnp.concatenate(
                    [value, jnp.broadcast_to(east[row : row + 1], (8, NZ))], axis=0
                )
            extent = value.shape[0]

            def directed(vectors):
                total = None
                for c in range(3):
                    s = lattice_speeds[q][c]
                    if s:
                        term = vectors[c][0:extent]
                        if total is None:
                            total = term if s > 0 else -term
                        else:
                            total = total + term if s > 0 else total - term
                return total

            balance = constant[0:extent]
            if q:
                cu = directed(flow)
                cf = directed(pull)
                balance = (
                    balance
                    + cu * (linear[0:extent] + quadratic[0:extent] * cu + (9.0 * gain) * cf)
                    + (3.0 * gain) * cf
                )
            post = (1.0 - rate) * value + lattice_weights[q] * balance
            if step_x:
                post = pltpu.roll(post, step_x % SX, 0)[0:WX]
            if step_z:
                post = pltpu.roll(post, step_z % NZ, 1)
            fresh[pl.ds(q * CELLS + y_to, WX, stride=WY), :] = post

    both = jnp.concatenate([z_high[...], z_high[...]], axis=0)
    rows = SY * SX
    for c in range(3):
        split = speed[c * rows : (c + 1) * rows].astype(bf16)
        value = jnp.dot(split, both, preferred_element_type=f32) + jnp.dot(
            split[:, 0:NZ], z_low[...], preferred_element_type=f32
        )
        sampled[c : c + 1] = jnp.sum(value * plane[...], axis=0, keepdims=True)


def call(kernel, outputs, scratch, name, operands, cost=None):
    return pl.pallas_call(
        kernel,
        out_shape=[jax.ShapeDtypeStruct(shape, kind) for shape, kind in outputs],
        in_specs=[pl.BlockSpec(memory_space=pltpu.VMEM)] * len(operands),
        out_specs=[pl.BlockSpec(memory_space=pltpu.VMEM)] * len(outputs),
        scratch_shapes=scratch,
        compiler_params=pltpu.CompilerParams(vmem_limit_bytes=32 * 1024 * 1024),
        name=name,
        cost_estimate=cost,
    )(*operands)


def shift(value, axis, step):
    size = lax.axis_size(axis)
    return lax.ppermute(value, axis, [(i, (i + step) % size) for i in range(size)])


def per_device(populations, vert_base, vert_frac, edges, stiffness, rest):
    pop = populations.reshape(19 * CELLS, NZ)
    cost = pl.CostEstimate(flops=1 << 30, bytes_accessed=1 << 23, transcendentals=0)
    (row,) = call(rows_kernel, [((TILE, NZ), jnp.int32)], [], "rows", [], cost)
    lanes, marks, plane = call(
        spread_kernel,
        [((SY * SX, NZ), f32), ((8, NZ), f32), ((SY * SX, VERTS), f32)],
        [],
        "spread",
        [vert_base, vert_frac, edges, stiffness.reshape(EDGES // NZ, NZ), rest, row],
    )
    moment, edge, up, down = call(
        strips_kernel,
        [((4 * CELLS, NZ), f32), ((48, NZ), f32), ((STRIP_ROWS, NZ), f32), ((STRIP_ROWS, NZ), f32)],
        [],
        "strips",
        [pop, lanes, marks],
    )
    below = shift(up, "gy", 1)
    above = shift(down, "gy", -1)
    force, z_high, z_low = call(
        tables_kernel,
        [((SY * 3 * SX, NZ), f32), ((NZ, VERTS), bf16), ((NZ, VERTS), bf16)],
        [],
        "tables",
        [vert_base, vert_frac, lanes, marks],
        cost,
    )
    force, right, left = call(
        merge_kernel,
        [((SY * 3 * SX, NZ), f32), ((SIDE_ROWS, NZ), f32), ((SIDE_ROWS, NZ), f32)],
        [],
        "merge",
        [force, moment, edge, below, above],
    )
    west = shift(right, "gx", 1)
    east = shift(left, "gx", -1)
    fresh, sampled = call(
        collide_kernel,
        [((19 * CELLS, NZ), f32), ((3, VERTS), f32)],
        [
            pltpu.VMEM((SY * 3 * SX, NZ), f32),
            pltpu.VMEM((SY * 4 * SX, NZ), f32),
            pltpu.VMEM((SY * 3 * SX, 2 * NZ), f32),
        ],
        "collide",
        [pop, force, moment, below, above, west, east, plane, z_high, z_low],
    )
    return fresh.reshape(19, WX, WY, NZ), sampled


def solution(mesh):
    placed = (
        P(None, "gx", "gy", None),
        P(None, ("gx", "gy")),
        P(None, ("gx", "gy")),
        P(None, ("gx", "gy")),
        P(("gx", "gy")),
        P(None, ("gx", "gy")),
    )
    return jax.shard_map(
        per_device,
        mesh=mesh,
        in_specs=placed,
        out_specs=(P(None, "gx", "gy", None), P(None, ("gx", "gy"))),
        check_vma=False,
    )
```

```python
import jax
import jax.numpy as jnp
from jax import lax
from jax.experimental import pallas as pl
from jax.experimental.pallas import tpu as pltpu
from jax.sharding import PartitionSpec as P

lattice_speeds = [
    (0, 0, 0),
    (1, 0, 0),
    (-1, 0, 0),
    (0, 1, 0),
    (0, -1, 0),
    (0, 0, 1),
    (0, 0, -1),
    (1, 1, 0),
    (-1, -1, 0),
    (1, -1, 0),
    (-1, 1, 0),
    (1, 0, 1),
    (-1, 0, -1),
    (1, 0, -1),
    (-1, 0, 1),
    (0, 1, 1),
    (0, -1, -1),
    (0, 1, -1),
    (0, -1, 1),
]
lattice_weights = [1.0 / 3.0] + [1.0 / 18.0] * 6 + [1.0 / 36.0] * 12
relax_time = 0.9

f32 = jnp.float32
bf16 = jnp.bfloat16

WX, WY, NZ = 16, 4, 128
CELLS = WX * WY
VERTS, TILE, EDGES = 512, 128, 1536
SX, SY = 24, 7

UP_Y = [q for q in range(19) if lattice_speeds[q][1] == 1]
DOWN_Y = [q for q in range(19) if lattice_speeds[q][1] == -1]
UP_X = [q for q in range(19) if lattice_speeds[q][0] == 1]
DOWN_X = [q for q in range(19) if lattice_speeds[q][0] == -1]

FORCE_ROWS = 64
MARK_ROW = 57
POP_ROWS = FORCE_ROWS + 4 * WX
UP_ROWS = POP_ROWS + 5 * WX
STRIP_ROWS = UP_ROWS + 4 * WX
SIDE_MOMENTS = 64
SIDE_DENSITY = 92
SIDE_POP = 100
SIDE_ROWS = 120
INNER = 13
RIM = (23, 0, 1, 15, 16, 17)


def outer_weight(r):
    return (5.0 - 2.0 * r - jnp.sqrt(-7.0 + 12.0 * r - 4.0 * r * r)) / 8.0


def inner_weight(r):
    return (3.0 - 2.0 * r + jnp.sqrt(1.0 + 4.0 * r - 4.0 * r * r)) / 8.0


def halves(value):
    high = value.astype(bf16)
    low = (value - high.astype(f32)).astype(bf16)
    return high, low


def along_last(a, b):
    return lax.dot_general(a, b, (((1,), (1,)), ((), ())), preferred_element_type=f32)


def iota(shape, dim):
    return lax.broadcasted_iota(jnp.int32, shape, dim)


def edge_forces(base, frac, edges, stiffness, rest, row):
    head = edges[0:1]
    tail = edges[1:2]
    run = head >> 7
    local = jnp.concatenate([row] * (EDGES // NZ), axis=1)
    plus = local == (tail & (TILE - 1))
    minus = local == (head & (TILE - 1))
    signed = jnp.where(plus, 1.0, jnp.where(minus, -1.0, 0.0)).astype(bf16)
    whole = base.astype(f32)
    high, low = halves(frac)
    blank = jnp.zeros((5, TILE), f32)
    pieces = []
    for part in (whole, high.astype(f32), low.astype(f32)):
        for t in range(4):
            pieces += [part[:, t * TILE : (t + 1) * TILE], blank]
    stacked = jnp.concatenate(pieces, axis=0).astype(bf16)
    found = jnp.dot(stacked, signed, preferred_element_type=f32)
    found = found[0:32] + found[32:64] + found[64:96]
    apart = jnp.zeros((8, EDGES), f32)
    for t in range(4):
        apart = apart + jnp.where(run == t, found[8 * t : 8 * t + 8], 0.0)
    stretch = stiffness * (apart[0:3] - rest)
    high, low = halves(stretch)
    blank = jnp.zeros((5, EDGES), f32)
    pieces = []
    for part in (high.astype(f32), low.astype(f32)):
        for t in range(4):
            pieces += [jnp.where(run == t, part, 0.0), blank]
    stacked = jnp.concatenate(pieces, axis=0).astype(bf16)
    pulled = along_last(stacked, signed)
    pulled = pulled[0:32] + pulled[32:64]
    return jnp.concatenate([-pulled[8 * t : 8 * t + 3] for t in range(4)], axis=1)


def rows_kernel(row):
    row[...] = iota((TILE, NZ), 0)


def kernel_of(frac):
    return [
        outer_weight(1.0 + frac),
        inner_weight(frac),
        inner_weight(1.0 - frac),
        outer_weight(2.0 - frac),
    ]


def columns(kernel, offset):
    total = jnp.where(offset == 0, kernel[0], 0.0)
    for step in range(1, 4):
        total = jnp.where(offset == step, kernel[step], total)
    return total


def windows(lanes, marks):
    component = (iota((1, TILE), 1) >> 3) & 3
    depth = iota((NZ, TILE), 0).astype(f32)
    match = jnp.where(depth == marks, 1.0, 0.0)
    spots = jnp.concatenate([jnp.where(component == c, match, 0.0) for c in range(3)], axis=0)
    high, low = halves(lanes)
    rows = lanes.shape[0]
    both = jnp.concatenate([high.astype(f32), low.astype(f32)], axis=0).astype(bf16)
    wide = along_last(both, spots.astype(bf16))
    return wide[0:rows] + wide[rows : 2 * rows]


def strip(out, lanes, marks, moment, pop, slab, dirs, edge_row):
    for k in range(3):
        out[k * WX : (k + 1) * WX] = lanes[(slab + k) * SX : (slab + k) * SX + WX]
    for n, x in enumerate((16, 17, 23)):
        out[48 + 3 * n : 51 + 3 * n] = lanes[pl.ds(slab * SX + x, 3, stride=SX), :]
    out[MARK_ROW:FORCE_ROWS] = jnp.broadcast_to(marks[0:1], (FORCE_ROWS - MARK_ROW, NZ))
    for q in range(4):
        at = FORCE_ROWS + q * WX
        out[at : at + WX] = moment[pl.ds(q * CELLS + edge_row, WX, stride=WY), :]
    for k, q in enumerate(dirs):
        at = POP_ROWS + k * WX
        out[at : at + WX] = pop[pl.ds(q * CELLS + edge_row, WX, stride=WY), :]


def spread_kernel(base, frac, edges, stiffness, rest, row, lanes, marks, inner_out, rim_out):
    springs = jnp.concatenate([stiffness[k : k + 1] for k in range(EDGES // NZ)], axis=1)
    membrane = edge_forces(base[...], frac[...], edges[...], springs, rest[...], row[...])
    part = frac[...]
    kernel = kernel_of(part)
    cell = base[...]

    slot = iota((SX, VERTS), 0)
    slot = jnp.where(slot == SX - 1, -1, slot)
    along_x = columns([k[0:1] for k in kernel], slot - (cell[0:1] & (WX - 1)) + 1)
    slab = iota((8, VERTS), 0)
    along_y = columns([k[1:2] for k in kernel], slab - (cell[1:2] & (WY - 1)))
    plane = jnp.concatenate([along_x * along_y[y : y + 1] for y in range(SY)], axis=0)
    inside = jnp.where(iota((WX, VERTS), 0) < INNER, along_x[2 : 2 + WX], 0.0)
    inner_out[...] = jnp.concatenate([inside * along_y[y : y + 1] for y in range(SY)], axis=0)
    rim_out[...] = jnp.concatenate([along_x[x : x + 1] * along_y for x in RIM], axis=0)

    layer = iota((8, TILE), 0)
    lane = iota((1, TILE), 1)
    mark = jnp.zeros((1, TILE), jnp.int32)
    blocks = []
    for t in range(4):
        span = slice(t * TILE, (t + 1) * TILE)
        z = cell[2:3, span]
        apart = ((z - z[:, 0:1] + 64) & (NZ - 1)) - 64
        lowest = jnp.min(apart.astype(f32), axis=1, keepdims=True).astype(jnp.int32)
        along_z = columns([k[2:3, span] for k in kernel], layer - apart + lowest)
        start = z[:, 0:1] + lowest - 1
        mark = jnp.where(lane >> 5 == t, (start + (lane & 7)) & (NZ - 1), mark)
        block = [along_z * membrane[c : c + 1, span] for c in range(3)] + [jnp.zeros((8, TILE), f32)]
        row_of = [jnp.zeros((32, TILE), f32)] * 4
        row_of[t] = jnp.concatenate(block, axis=0)
        blocks.append(jnp.concatenate(row_of, axis=1))
    loaded = jnp.concatenate(blocks, axis=0)
    marks[...] = jnp.broadcast_to(mark.astype(f32), (8, TILE))
    plane_high, plane_low = halves(plane)
    load_high, load_low = halves(loaded)
    lanes[...] = (
        along_last(plane_high, load_high)
        + along_last(plane_low, load_high)
        + along_last(plane_high, load_low)
    )


def strips_kernel(pop, lanes, marks, moment, edge_out, up, down):
    density = pop[0:CELLS]
    moments = [None, None, None]
    for q in range(1, 19):
        value = pop[q * CELLS : (q + 1) * CELLS]
        density = density + value
        for d in range(3):
            c = lattice_speeds[q][d]
            if c:
                if moments[d] is None:
                    moments[d] = value if c > 0 else -value
                else:
                    moments[d] = moments[d] + value if c > 0 else moments[d] - value
    moment[0:CELLS] = density
    for d in range(3):
        moment[(d + 1) * CELLS : (d + 2) * CELLS] = moments[d]
    strip(up, lanes, marks, moment, pop, 4, UP_Y, 3)
    strip(down, lanes, marks, moment, pop, 0, DOWN_Y, 0)
    for q in range(4):
        at = UP_ROWS + q * WX
        down[at : at + WX] = moment[pl.ds(q * CELLS + 1, WX, stride=WY), :]
    for k, q in enumerate(UP_X):
        edge_out[k * 4 : k * 4 + 4] = pop[q * CELLS + 60 : q * CELLS + 64]
    for k, q in enumerate(DOWN_X):
        edge_out[24 + k * 4 : 24 + k * 4 + 4] = pop[q * CELLS : q * CELLS + 4]


def tables_kernel(base, frac, lanes, marks, force, high_out, low_out):
    wide = windows(lanes[...], marks[0:1])
    for slab in range(SY):
        for c in range(3):
            row = (slab * 3 + c) * SX
            force[row : row + SX] = wide[slab * SX : (slab + 1) * SX, c * NZ : (c + 1) * NZ]
    kernel = kernel_of(frac[2:3])
    depth = iota((NZ, VERTS), 0)
    along_z = columns(kernel, (depth - base[2:3] + 1) & (NZ - 1))
    z_high, z_low = halves(along_z)
    high_out[...] = z_high
    low_out[...] = z_low


def outgoing(out, force, moment, edge, below, above, sources, x, behind, offset, dirs):
    def moments_at(x, y, first):
        count = 4 - first
        if y < 0:
            return below[pl.ds(FORCE_ROWS + first * WX + x, count, stride=WX), :]
        if y < 4:
            return moment[pl.ds(first * CELLS + x * 4 + y, count, stride=CELLS), :]
        at = FORCE_ROWS if y == 4 else UP_ROWS
        return above[pl.ds(at + first * WX + x, count, stride=WX), :]

    for n, source in enumerate(sources):
        if source == behind:
            for y in range(SY):
                value = force[pl.ds(y * 3 * SX + source, 3, stride=SX), :]
                value = value + 2.0 * moments_at(source, y - 1, 1)
                out[21 * n + 3 * y : 21 * n + 3 * y + 3] = value
                out[SIDE_DENSITY + y : SIDE_DENSITY + y + 1] = moments_at(source, y - 1, 0)[0:1]
        else:
            out[21 * n : 21 * n + 21] = force[pl.ds(source, 21, stride=SX), :]
    for y in range(SY):
        out[SIDE_MOMENTS + 4 * y : SIDE_MOMENTS + 4 * y + 4] = moments_at(x, y - 1, 0)
    at = SIDE_POP
    for k, q in enumerate(dirs):
        row = offset + k * 4
        step = lattice_speeds[q][1]
        if step == 0:
            out[at : at + 4] = edge[row : row + 4]
        elif step == 1:
            source = POP_ROWS + UP_Y.index(q) * WX + x
            out[at : at + 1] = below[source : source + 1]
            out[at + 1 : at + 4] = edge[row : row + 3]
        else:
            source = POP_ROWS + DOWN_Y.index(q) * WX + x
            out[at : at + 3] = edge[row + 1 : row + 4]
            out[at + 3 : at + 4] = above[source : source + 1]
        at += 4


def merge_kernel(force_in, moment, edge, below, above, force, right, left):
    for row in range(0, SY * 3 * SX, SX):
        force[row : row + SX] = force_in[row : row + SX]
    for block, slab in ((below, 0), (above, 4)):
        wide = windows(block[0:FORCE_ROWS], block[MARK_ROW : MARK_ROW + 1])
        for c in range(3):
            part = wide[:, c * NZ : (c + 1) * NZ]
            for k in range(3):
                row = ((slab + k) * 3 + c) * SX
                force[row : row + WX] = force[row : row + WX] + part[k * WX : (k + 1) * WX]
            for n, x in enumerate((16, 17, 23)):
                rows = pl.ds((slab * 3 + c) * SX + x, 3, stride=3 * SX)
                force[rows, :] = force[rows, :] + part[48 + 3 * n : 51 + 3 * n]
    outgoing(right, force, moment, edge, below, above, (15, 16, 17), 15, None, 0, UP_X)
    outgoing(left, force, moment, edge, below, above, (23, 0, 1), 0, 1, 24, DOWN_X)


def collide(density, momentum, pull):
    rate = 1.0 / relax_time
    gain = 1.0 - 0.5 / relax_time
    inverse = 1.0 / density
    flow = [(momentum[c] + 0.5 * pull[c]) * inverse for c in range(3)]
    square = flow[0] * flow[0] + flow[1] * flow[1] + flow[2] * flow[2]
    work = flow[0] * pull[0] + flow[1] * pull[1] + flow[2] * pull[2]
    scaled = rate * density
    constant = scaled * (1.0 - 1.5 * square) - (3.0 * gain) * work
    linear = 3.0 * scaled
    quadratic = 4.5 * scaled

    def directed(vectors, q):
        total = None
        for c in range(3):
            s = lattice_speeds[q][c]
            if s:
                if total is None:
                    total = vectors[c] if s > 0 else -vectors[c]
                else:
                    total = total + vectors[c] if s > 0 else total - vectors[c]
        return total

    def gained(q):
        if q == 0:
            return lattice_weights[0] * constant
        cu = directed(flow, q)
        cf = directed(pull, q)
        balance = constant + cu * (linear + quadratic * cu + (9.0 * gain) * cf) + (3.0 * gain) * cf
        return lattice_weights[q] * balance

    return flow, gained


def moved_z(post, q):
    step = lattice_speeds[q][2]
    return pltpu.roll(post, step % NZ, 1) if step else post


def sample(speeds, plane, z_high, z_low):
    high, low = halves(speeds)
    split = jnp.concatenate([high.astype(f32), low.astype(f32)], axis=1).astype(bf16)
    both = jnp.concatenate([z_high, z_high], axis=0)
    value = jnp.dot(split, both, preferred_element_type=f32)
    value = value + jnp.dot(high, z_low, preferred_element_type=f32)
    return jnp.sum(value * plane, axis=0, keepdims=True)


def inner_kernel(pop, force, moment, below, above, plane, z_high, z_low, fresh, kept, sampled, speed):
    left = 1.0 - 1.0 / relax_time
    for slab in range(SY):
        y_from = slab - 1
        known = []
        for q in range(4):
            if slab == 0:
                at = FORCE_ROWS + q * WX + 2
                known.append(below[at : at + INNER])
            elif slab < 5:
                known.append(moment[pl.ds(q * CELLS + 2 * WY + y_from, INNER, stride=WY), :])
            else:
                at = (FORCE_ROWS if slab == 5 else UP_ROWS) + q * WX + 2
                known.append(above[at : at + INNER])
        pull = []
        for c in range(3):
            row = (slab * 3 + c) * SX + 2
            pull.append(force[row : row + INNER])
        flow, gained = collide(known[0], known[1:], pull)
        for c in range(3):
            row = (c * SY + slab) * WX
            speed[row : row + WX] = jnp.concatenate([flow[c], jnp.zeros((3, NZ), f32)], axis=0)
        for q in range(19):
            step_x, step_y, _ = lattice_speeds[q]
            y_to = y_from + step_y
            if y_from == 5 or y_to < 0 or y_to > 3:
                continue
            if 0 <= y_from <= 3:
                value = pop[pl.ds(q * CELLS + 2 * WY + y_from, INNER, stride=WY), :]
            elif y_from < 0:
                at = POP_ROWS + UP_Y.index(q) * WX + 2
                value = below[at : at + INNER]
            else:
                at = POP_ROWS + DOWN_Y.index(q) * WX + 2
                value = above[at : at + INNER]
            post = moved_z(left * value + gained(q), q)
            fresh[pl.ds(q * CELLS + (2 + step_x) * WY + y_to, INNER, stride=WY), :] = post
    for q in range(19):
        for n, x in enumerate(KEPT[lattice_speeds[q][0]]):
            at = q * CELLS + x * WY
            kept[q, n] = fresh[at : at + WY]
    rows = SY * WX
    for c in range(3):
        sampled[c : c + 1] = sample(speed[c * rows : (c + 1) * rows], plane[...], z_high[...], z_low[...])


KEPT = {0: (2, 14), 1: (14, 15), -1: (1, 2)}


def rim_kernel(
    fresh_in,
    kept,
    part,
    pop,
    force,
    moment,
    below,
    above,
    west,
    east,
    plane,
    z_high,
    z_low,
    fresh,
    sampled_far,
    low_side,
    high_side,
    sampled,
    sent,
):
    left = 1.0 - 1.0 / relax_time
    speeds = [[], [], []]
    for n, slot in enumerate(RIM):
        x = -1 if slot == 23 else slot
        side = west if n < 3 else east
        pull = []
        for c in range(3):
            value = force[pl.ds(c * SX + slot, SY, stride=3 * SX), :]
            value = value + side[pl.ds(21 * (n % 3) + c, SY, stride=3), :]
            pull.append(jnp.concatenate([value, jnp.zeros((1, NZ), f32)], axis=0))
        known = []
        for q in range(4):
            fill = jnp.full((1, NZ), 0.0 if q else 1.0, f32)
            if x in (-1, 16):
                rows = [side[pl.ds(SIDE_MOMENTS + q, SY, stride=4), :], fill]
            elif x == 17:
                if q:
                    rows = [jnp.zeros((8, NZ), f32)]
                else:
                    rows = [side[SIDE_DENSITY : SIDE_DENSITY + SY], fill]
            else:
                near, far = FORCE_ROWS + q * WX + x, UP_ROWS + q * WX + x
                own = q * CELLS + x * WY
                rows = [below[near : near + 1], moment[own : own + WY], above[near : near + 1], above[far : far + 1], fill]
            known.append(jnp.concatenate(rows, axis=0) if len(rows) > 1 else rows[0])
        flow, gained = collide(known[0], known[1:], pull)
        for c in range(3):
            speeds[c].append(flow[c])
        for q in range(19):
            step_x, step_y, _ = lattice_speeds[q]
            x_to = x + step_x
            if x_to not in (0, 1, 2, 14, 15) or (x == 15 and step_x == 1) or x == 17:
                continue
            own = q * CELLS + x * WY
            if x in (-1, 16):
                at = SIDE_POP + (UP_X if x < 0 else DOWN_X).index(q) * 4
                value = side[at : at + 4]
            elif step_y == 0:
                value = pop[own : own + 4]
            elif step_y == 1:
                at = POP_ROWS + UP_Y.index(q) * WX + x
                value = jnp.concatenate([below[at : at + 1], pop[own : own + 3]], axis=0)
            else:
                at = POP_ROWS + DOWN_Y.index(q) * WX + x
                value = jnp.concatenate([pop[own + 1 : own + 4], above[at : at + 1]], axis=0)
            post = moved_z(left * value + gained(q)[1 - step_y : 5 - step_y], q)
            if x_to < 3:
                low_side[q, x_to] = post
            else:
                high_side[q, x_to - 14] = post
    for q in range(19):
        for n, x in enumerate(KEPT[lattice_speeds[q][0]]):
            if x < 3:
                low_side[q, x] = kept[q, n]
            else:
                high_side[q, x - 14] = kept[q, n]
    copies = [
        pltpu.make_async_copy(low_side, fresh.at[:, 0:3], sent.at[0]),
        pltpu.make_async_copy(high_side, fresh.at[:, 14:16], sent.at[1]),
    ]
    for copy in copies:
        copy.start()
    for c in range(3):
        total = sample(jnp.concatenate(speeds[c], axis=0), plane[...], z_high[...], z_low[...])
        sampled[c : c + 1] = part[c : c + 1] + total
    last = pltpu.make_async_copy(sampled, sampled_far, sent.at[2])
    last.start()
    for copy in copies:
        copy.wait()
    last.wait()


def call(kernel, outputs, scratch, name, operands, cost=None):
    return pl.pallas_call(
        kernel,
        out_shape=[jax.ShapeDtypeStruct(shape, kind) for shape, kind in outputs],
        in_specs=[pl.BlockSpec(memory_space=pltpu.VMEM)] * len(operands),
        out_specs=[pl.BlockSpec(memory_space=pltpu.VMEM)] * len(outputs),
        scratch_shapes=scratch,
        compiler_params=pltpu.CompilerParams(vmem_limit_bytes=32 * 1024 * 1024),
        name=name,
        cost_estimate=cost,
    )(*operands)


def shift(value, axis, step):
    size = lax.axis_size(axis)
    return lax.ppermute(value, axis, [(i, (i + step) % size) for i in range(size)])


def per_device(populations, vert_base, vert_frac, edges, stiffness, rest):
    pop = populations.reshape(19 * CELLS, NZ)
    cost = pl.CostEstimate(flops=1 << 30, bytes_accessed=1 << 23, transcendentals=0)
    (row,) = call(rows_kernel, [((TILE, NZ), jnp.int32)], [], "rows", [], cost)
    lanes, marks, inner_plane, rim_plane = call(
        spread_kernel,
        [((SY * SX, NZ), f32), ((8, NZ), f32), ((SY * WX, VERTS), f32), ((48, VERTS), f32)],
        [],
        "spread",
        [vert_base, vert_frac, edges, stiffness.reshape(EDGES // NZ, NZ), rest, row],
    )
    moment, edge, up, down = call(
        strips_kernel,
        [((4 * CELLS, NZ), f32), ((48, NZ), f32), ((STRIP_ROWS, NZ), f32), ((STRIP_ROWS, NZ), f32)],
        [],
        "strips",
        [pop, lanes, marks],
    )
    below = shift(up, "gy", 1)
    above = shift(down, "gy", -1)
    force, z_high, z_low = call(
        tables_kernel,
        [((SY * 3 * SX, NZ), f32), ((NZ, VERTS), bf16), ((NZ, VERTS), bf16)],
        [],
        "tables",
        [vert_base, vert_frac, lanes, marks],
        cost,
    )
    force, right, left = call(
        merge_kernel,
        [((SY * 3 * SX, NZ), f32), ((SIDE_ROWS, NZ), f32), ((SIDE_ROWS, NZ), f32)],
        [],
        "merge",
        [force, moment, edge, below, above],
    )
    west = shift(right, "gx", 1)
    east = shift(left, "gx", -1)
    fresh, kept, part = call(
        inner_kernel,
        [((19 * CELLS, NZ), f32), ((19, 2, WY, NZ), f32), ((3, VERTS), f32)],
        [pltpu.VMEM((3 * SY * WX, NZ), f32)],
        "inner",
        [pop, force, moment, below, above, inner_plane, z_high, z_low],
        cost,
    )
    vmem = pl.BlockSpec(memory_space=pltpu.VMEM)
    far = pl.BlockSpec(memory_space=pltpu.HBM)
    return pl.pallas_call(
        rim_kernel,
        out_shape=[
            jax.ShapeDtypeStruct((19, WX, WY, NZ), f32),
            jax.ShapeDtypeStruct((3, VERTS), f32),
        ],
        in_specs=[far] + [vmem] * 12,
        out_specs=[far, far],
        scratch_shapes=[
            pltpu.VMEM((19, 3, WY, NZ), f32),
            pltpu.VMEM((19, 2, WY, NZ), f32),
            pltpu.VMEM((3, VERTS), f32),
            pltpu.SemaphoreType.DMA((3,)),
        ],
        input_output_aliases={0: 0},
        compiler_params=pltpu.CompilerParams(vmem_limit_bytes=32 * 1024 * 1024),
        name="rim",
    )(
        fresh.reshape(19, WX, WY, NZ),
        kept,
        part,
        pop,
        force,
        moment,
        below,
        above,
        west,
        east,
        rim_plane,
        z_high,
        z_low,
    )


def solution(mesh):
    placed = (
        P(None, "gx", "gy", None),
        P(None, ("gx", "gy")),
        P(None, ("gx", "gy")),
        P(None, ("gx", "gy")),
        P(("gx", "gy")),
        P(None, ("gx", "gy")),
    )
    return jax.shard_map(
        per_device,
        mesh=mesh,
        in_specs=placed,
        out_specs=(P(None, "gx", "gy", None), P(None, ("gx", "gy"))),
        check_vma=False,
    )
```

```python
import jax
import jax.numpy as jnp
from jax import lax
from jax.experimental import pallas as pl
from jax.experimental.pallas import tpu as pltpu
from jax.sharding import PartitionSpec as P

lattice_speeds = [
    (0, 0, 0),
    (1, 0, 0),
    (-1, 0, 0),
    (0, 1, 0),
    (0, -1, 0),
    (0, 0, 1),
    (0, 0, -1),
    (1, 1, 0),
    (-1, -1, 0),
    (1, -1, 0),
    (-1, 1, 0),
    (1, 0, 1),
    (-1, 0, -1),
    (1, 0, -1),
    (-1, 0, 1),
    (0, 1, 1),
    (0, -1, -1),
    (0, 1, -1),
    (0, -1, 1),
]
lattice_weights = [1.0 / 3.0] + [1.0 / 18.0] * 6 + [1.0 / 36.0] * 12
relax_time = 0.9

f32 = jnp.float32
bf16 = jnp.bfloat16

WX, WY, NZ = 16, 4, 128
CELLS = WX * WY
VERTS, TILE, EDGES = 512, 128, 1536
SX, SY = 24, 7

UP_Y = [q for q in range(19) if lattice_speeds[q][1] == 1]
DOWN_Y = [q for q in range(19) if lattice_speeds[q][1] == -1]
UP_X = [q for q in range(19) if lattice_speeds[q][0] == 1]
DOWN_X = [q for q in range(19) if lattice_speeds[q][0] == -1]

FORCE_ROWS = 64
MARK_ROW = 57
POP_ROWS = FORCE_ROWS + 4 * WX
UP_ROWS = POP_ROWS + 5 * WX
STRIP_ROWS = UP_ROWS + 4 * WX
SIDE_MOMENTS = 64
SIDE_DENSITY = 92
SIDE_POP = 100
SIDE_ROWS = 120
INNER = 13
RIM = (23, 0, 1, 15, 16, 17)


def outer_weight(r):
    return (5.0 - 2.0 * r - jnp.sqrt(-7.0 + 12.0 * r - 4.0 * r * r)) / 8.0


def inner_weight(r):
    return (3.0 - 2.0 * r + jnp.sqrt(1.0 + 4.0 * r - 4.0 * r * r)) / 8.0


def halves(value):
    high = value.astype(bf16)
    low = (value - high.astype(f32)).astype(bf16)
    return high, low


def along_last(a, b):
    return lax.dot_general(a, b, (((1,), (1,)), ((), ())), preferred_element_type=f32)


def iota(shape, dim):
    return lax.broadcasted_iota(jnp.int32, shape, dim)


def edge_forces(base, frac, edges, stiffness, rest, row):
    head = edges[0:1]
    tail = edges[1:2]
    run = head >> 7
    local = jnp.concatenate([row] * (EDGES // NZ), axis=1)
    plus = local == (tail & (TILE - 1))
    minus = local == (head & (TILE - 1))
    signed = jnp.where(plus, 1.0, jnp.where(minus, -1.0, 0.0)).astype(bf16)
    whole = base.astype(f32)
    high, low = halves(frac)
    blank = jnp.zeros((5, TILE), f32)
    pieces = []
    for part in (whole, high.astype(f32), low.astype(f32)):
        for t in range(4):
            pieces += [part[:, t * TILE : (t + 1) * TILE], blank]
    stacked = jnp.concatenate(pieces, axis=0).astype(bf16)
    found = jnp.dot(stacked, signed, preferred_element_type=f32)
    found = found[0:32] + found[32:64] + found[64:96]
    apart = jnp.zeros((8, EDGES), f32)
    for t in range(4):
        apart = apart + jnp.where(run == t, found[8 * t : 8 * t + 8], 0.0)
    stretch = stiffness * (apart[0:3] - rest)
    high, low = halves(stretch)
    blank = jnp.zeros((5, EDGES), f32)
    pieces = []
    for part in (high.astype(f32), low.astype(f32)):
        for t in range(4):
            pieces += [jnp.where(run == t, part, 0.0), blank]
    stacked = jnp.concatenate(pieces, axis=0).astype(bf16)
    pulled = along_last(stacked, signed)
    pulled = pulled[0:32] + pulled[32:64]
    return jnp.concatenate([-pulled[8 * t : 8 * t + 3] for t in range(4)], axis=1)


def rows_kernel(row):
    row[...] = iota((TILE, NZ), 0)


def kernel_of(frac):
    return [
        outer_weight(1.0 + frac),
        inner_weight(frac),
        inner_weight(1.0 - frac),
        outer_weight(2.0 - frac),
    ]


def columns(kernel, offset):
    total = jnp.where(offset == 0, kernel[0], 0.0)
    for step in range(1, 4):
        total = jnp.where(offset == step, kernel[step], total)
    return total


def windows(lanes, marks):
    component = (iota((1, TILE), 1) >> 3) & 3
    depth = iota((NZ, TILE), 0).astype(f32)
    match = jnp.where(depth == marks, 1.0, 0.0)
    spots = jnp.concatenate([jnp.where(component == c, match, 0.0) for c in range(3)], axis=0)
    high, low = halves(lanes)
    rows = lanes.shape[0]
    both = jnp.concatenate([high.astype(f32), low.astype(f32)], axis=0).astype(bf16)
    wide = along_last(both, spots.astype(bf16))
    return wide[0:rows] + wide[rows : 2 * rows]


def strip(out, lanes, marks, moment, pop, slab, dirs, edge_row):
    for k in range(3):
        out[k * WX : (k + 1) * WX] = lanes[(slab + k) * SX : (slab + k) * SX + WX]
    for n, x in enumerate((16, 17, 23)):
        out[48 + 3 * n : 51 + 3 * n] = lanes[pl.ds(slab * SX + x, 3, stride=SX), :]
    out[MARK_ROW:FORCE_ROWS] = jnp.broadcast_to(marks[0:1], (FORCE_ROWS - MARK_ROW, NZ))
    for q in range(4):
        at = FORCE_ROWS + q * WX
        out[at : at + WX] = moment[pl.ds(q * CELLS + edge_row, WX, stride=WY), :]
    for k, q in enumerate(dirs):
        at = POP_ROWS + k * WX
        out[at : at + WX] = pop[pl.ds(q * CELLS + edge_row, WX, stride=WY), :]


def spread_kernel(base, frac, edges, stiffness, rest, row, lanes, marks, inner_out, rim_out):
    springs = jnp.concatenate([stiffness[k : k + 1] for k in range(EDGES // NZ)], axis=1)
    membrane = edge_forces(base[...], frac[...], edges[...], springs, rest[...], row[...])
    part = frac[...]
    kernel = kernel_of(part)
    cell = base[...]

    slot = iota((SX, VERTS), 0)
    slot = jnp.where(slot == SX - 1, -1, slot)
    along_x = columns([k[0:1] for k in kernel], slot - (cell[0:1] & (WX - 1)) + 1)
    slab = iota((8, VERTS), 0)
    along_y = columns([k[1:2] for k in kernel], slab - (cell[1:2] & (WY - 1)))
    plane = jnp.concatenate([along_x * along_y[y : y + 1] for y in range(SY)], axis=0)
    inside = jnp.where(iota((WX, VERTS), 0) < INNER, along_x[2 : 2 + WX], 0.0)
    inner_out[...] = jnp.concatenate([inside * along_y[y : y + 1] for y in range(SY)], axis=0)
    rim_out[...] = jnp.concatenate([along_x[x : x + 1] * along_y for x in RIM], axis=0)

    layer = iota((8, TILE), 0)
    lane = iota((1, TILE), 1)
    mark = jnp.zeros((1, TILE), jnp.int32)
    blocks = []
    for t in range(4):
        span = slice(t * TILE, (t + 1) * TILE)
        z = cell[2:3, span]
        apart = ((z - z[:, 0:1] + 64) & (NZ - 1)) - 64
        lowest = jnp.min(apart.astype(f32), axis=1, keepdims=True).astype(jnp.int32)
        along_z = columns([k[2:3, span] for k in kernel], layer - apart + lowest)
        start = z[:, 0:1] + lowest - 1
        mark = jnp.where(lane >> 5 == t, (start + (lane & 7)) & (NZ - 1), mark)
        block = [along_z * membrane[c : c + 1, span] for c in range(3)] + [jnp.zeros((8, TILE), f32)]
        row_of = [jnp.zeros((32, TILE), f32)] * 4
        row_of[t] = jnp.concatenate(block, axis=0)
        blocks.append(jnp.concatenate(row_of, axis=1))
    loaded = jnp.concatenate(blocks, axis=0)
    marks[...] = jnp.broadcast_to(mark.astype(f32), (8, TILE))
    plane_high, plane_low = halves(plane)
    load_high, load_low = halves(loaded)
    lanes[...] = (
        along_last(plane_high, load_high)
        + along_last(plane_low, load_high)
        + along_last(plane_high, load_low)
    )


def strips_kernel(pop, lanes, marks, moment, edge_out, up, down):
    density = pop[0:CELLS]
    moments = [None, None, None]
    for q in range(1, 19):
        value = pop[q * CELLS : (q + 1) * CELLS]
        density = density + value
        for d in range(3):
            c = lattice_speeds[q][d]
            if c:
                if moments[d] is None:
                    moments[d] = value if c > 0 else -value
                else:
                    moments[d] = moments[d] + value if c > 0 else moments[d] - value
    moment[0:CELLS] = density
    for d in range(3):
        moment[(d + 1) * CELLS : (d + 2) * CELLS] = moments[d]
    strip(up, lanes, marks, moment, pop, 4, UP_Y, 3)
    strip(down, lanes, marks, moment, pop, 0, DOWN_Y, 0)
    for q in range(4):
        at = UP_ROWS + q * WX
        down[at : at + WX] = moment[pl.ds(q * CELLS + 1, WX, stride=WY), :]
    for k, q in enumerate(UP_X):
        edge_out[k * 4 : k * 4 + 4] = pop[q * CELLS + 60 : q * CELLS + 64]
    for k, q in enumerate(DOWN_X):
        edge_out[24 + k * 4 : 24 + k * 4 + 4] = pop[q * CELLS : q * CELLS + 4]


def tables_kernel(base, frac, lanes, marks, force, high_out, low_out):
    wide = windows(lanes[...], marks[0:1])
    for slab in range(SY):
        for c in range(3):
            row = (slab * 3 + c) * SX
            force[row : row + SX] = wide[slab * SX : (slab + 1) * SX, c * NZ : (c + 1) * NZ]
    kernel = kernel_of(frac[2:3])
    depth = iota((NZ, VERTS), 0)
    along_z = columns(kernel, (depth - base[2:3] + 1) & (NZ - 1))
    z_high, z_low = halves(along_z)
    high_out[...] = z_high
    low_out[...] = z_low


def outgoing(out, force, moment, edge, below, above, sources, x, behind, offset, dirs):
    def moments_at(x, y, first):
        count = 4 - first
        if y < 0:
            return below[pl.ds(FORCE_ROWS + first * WX + x, count, stride=WX), :]
        if y < 4:
            return moment[pl.ds(first * CELLS + x * 4 + y, count, stride=CELLS), :]
        at = FORCE_ROWS if y == 4 else UP_ROWS
        return above[pl.ds(at + first * WX + x, count, stride=WX), :]

    for n, source in enumerate(sources):
        if source == behind:
            for y in range(SY):
                value = force[pl.ds(y * 3 * SX + source, 3, stride=SX), :]
                value = value + 2.0 * moments_at(source, y - 1, 1)
                out[21 * n + 3 * y : 21 * n + 3 * y + 3] = value
                out[SIDE_DENSITY + y : SIDE_DENSITY + y + 1] = moments_at(source, y - 1, 0)[0:1]
        else:
            out[21 * n : 21 * n + 21] = force[pl.ds(source, 21, stride=SX), :]
    for y in range(SY):
        out[SIDE_MOMENTS + 4 * y : SIDE_MOMENTS + 4 * y + 4] = moments_at(x, y - 1, 0)
    at = SIDE_POP
    for k, q in enumerate(dirs):
        row = offset + k * 4
        step = lattice_speeds[q][1]
        if step == 0:
            out[at : at + 4] = edge[row : row + 4]
        elif step == 1:
            source = POP_ROWS + UP_Y.index(q) * WX + x
            out[at : at + 1] = below[source : source + 1]
            out[at + 1 : at + 4] = edge[row : row + 3]
        else:
            source = POP_ROWS + DOWN_Y.index(q) * WX + x
            out[at : at + 3] = edge[row + 1 : row + 4]
            out[at + 3 : at + 4] = above[source : source + 1]
        at += 4


def merge_kernel(force, moment, edge, below, above, right, left, picked):
    outgoing(right, force, moment, edge, below, above, (15, 16, 17), 15, None, 0, UP_X)
    outgoing(left, force, moment, edge, below, above, (23, 0, 1), 0, 1, 24, DOWN_X)
    picked[...] = jnp.zeros((24, NZ), f32)
    for block, slab in ((below, 0), (above, 4)):
        for n, x in enumerate((0, 1, 15)):
            picked[3 * n : 3 * n + 3] = block[pl.ds(x, 3, stride=WX), :]
        picked[9:18] = block[48:57]
        wide = windows(picked[...], block[MARK_ROW : MARK_ROW + 1])
        for c in range(3):
            for n, (out, place) in enumerate(((left, 1), (left, 2), (right, 0), (right, 1), (right, 2), (left, 0))):
                rows = pl.ds(21 * place + 3 * slab + c, 3, stride=3)
                out[rows, :] = out[rows, :] + wide[3 * n : 3 * n + 3, c * NZ : (c + 1) * NZ]


def whole_force(force, force_in, below, above):
    for row in range(0, SY * 3 * SX, SX):
        force[row : row + SX] = force_in[row : row + SX]
    for block, slab in ((below, 0), (above, 4)):
        wide = windows(block[0:FORCE_ROWS], block[MARK_ROW : MARK_ROW + 1])
        for c in range(3):
            part = wide[:, c * NZ : (c + 1) * NZ]
            for k in range(3):
                row = ((slab + k) * 3 + c) * SX
                force[row : row + WX] = force[row : row + WX] + part[k * WX : (k + 1) * WX]
            for n, x in enumerate((16, 17, 23)):
                rows = pl.ds((slab * 3 + c) * SX + x, 3, stride=3 * SX)
                force[rows, :] = force[rows, :] + part[48 + 3 * n : 51 + 3 * n]


def collide(density, momentum, pull):
    rate = 1.0 / relax_time
    gain = 1.0 - 0.5 / relax_time
    inverse = 1.0 / density
    flow = [(momentum[c] + 0.5 * pull[c]) * inverse for c in range(3)]
    square = flow[0] * flow[0] + flow[1] * flow[1] + flow[2] * flow[2]
    work = flow[0] * pull[0] + flow[1] * pull[1] + flow[2] * pull[2]
    scaled = rate * density
    constant = scaled * (1.0 - 1.5 * square) - (3.0 * gain) * work
    linear = 3.0 * scaled
    quadratic = 4.5 * scaled

    def directed(vectors, q):
        total = None
        for c in range(3):
            s = lattice_speeds[q][c]
            if s:
                if total is None:
                    total = vectors[c] if s > 0 else -vectors[c]
                else:
                    total = total + vectors[c] if s > 0 else total - vectors[c]
        return total

    def gained(q):
        if q == 0:
            return lattice_weights[0] * constant
        cu = directed(flow, q)
        cf = directed(pull, q)
        balance = constant + cu * (linear + quadratic * cu + (9.0 * gain) * cf) + (3.0 * gain) * cf
        return lattice_weights[q] * balance

    return flow, gained


def moved_z(post, q):
    step = lattice_speeds[q][2]
    return pltpu.roll(post, step % NZ, 1) if step else post


def sample(speeds, plane, z_high, z_low):
    high, low = halves(speeds)
    split = jnp.concatenate([high.astype(f32), low.astype(f32)], axis=1).astype(bf16)
    both = jnp.concatenate([z_high, z_high], axis=0)
    value = jnp.dot(split, both, preferred_element_type=f32)
    value = value + jnp.dot(high, z_low, preferred_element_type=f32)
    return jnp.sum(value * plane, axis=0, keepdims=True)


def inner_kernel(
    pop, force_in, moment, below, above, plane, z_high, z_low, fresh, kept, sampled, force, speed
):
    whole_force(force, force_in, below, above)
    left = 1.0 - 1.0 / relax_time
    for slab in range(SY):
        y_from = slab - 1
        known = []
        for q in range(4):
            if slab == 0:
                at = FORCE_ROWS + q * WX + 2
                known.append(below[at : at + INNER])
            elif slab < 5:
                known.append(moment[pl.ds(q * CELLS + 2 * WY + y_from, INNER, stride=WY), :])
            else:
                at = (FORCE_ROWS if slab == 5 else UP_ROWS) + q * WX + 2
                known.append(above[at : at + INNER])
        pull = []
        for c in range(3):
            row = (slab * 3 + c) * SX + 2
            pull.append(force[row : row + INNER])
        flow, gained = collide(known[0], known[1:], pull)
        for c in range(3):
            row = (c * SY + slab) * WX
            speed[row : row + WX] = jnp.concatenate([flow[c], jnp.zeros((3, NZ), f32)], axis=0)
        for q in range(19):
            step_x, step_y, _ = lattice_speeds[q]
            y_to = y_from + step_y
            if y_from == 5 or y_to < 0 or y_to > 3:
                continue
            if 0 <= y_from <= 3:
                value = pop[pl.ds(q * CELLS + 2 * WY + y_from, INNER, stride=WY), :]
            elif y_from < 0:
                at = POP_ROWS + UP_Y.index(q) * WX + 2
                value = below[at : at + INNER]
            else:
                at = POP_ROWS + DOWN_Y.index(q) * WX + 2
                value = above[at : at + INNER]
            post = moved_z(left * value + gained(q), q)
            fresh[pl.ds(q * CELLS + (2 + step_x) * WY + y_to, INNER, stride=WY), :] = post
    for q in range(19):
        for n, x in enumerate(KEPT[lattice_speeds[q][0]]):
            at = q * CELLS + x * WY
            kept[q, n] = fresh[at : at + WY]
    rows = SY * WX
    for c in range(3):
        sampled[c : c + 1] = sample(speed[c * rows : (c + 1) * rows], plane[...], z_high[...], z_low[...])


KEPT = {0: (2, 14), 1: (14, 15), -1: (1, 2)}


def rim_kernel(
    fresh_in,
    kept,
    part,
    pop,
    force,
    moment,
    below,
    above,
    west,
    east,
    plane,
    z_high,
    z_low,
    fresh,
    sampled_far,
    low_side,
    high_side,
    sampled,
    sent,
):
    left = 1.0 - 1.0 / relax_time
    speeds = [[], [], []]
    for n, slot in enumerate(RIM):
        x = -1 if slot == 23 else slot
        side = west if n < 3 else east
        pull = []
        for c in range(3):
            value = force[pl.ds(c * SX + slot, SY, stride=3 * SX), :]
            value = value + side[pl.ds(21 * (n % 3) + c, SY, stride=3), :]
            pull.append(jnp.concatenate([value, jnp.zeros((1, NZ), f32)], axis=0))
        known = []
        for q in range(4):
            fill = jnp.full((1, NZ), 0.0 if q else 1.0, f32)
            if x in (-1, 16):
                rows = [side[pl.ds(SIDE_MOMENTS + q, SY, stride=4), :], fill]
            elif x == 17:
                if q:
                    rows = [jnp.zeros((8, NZ), f32)]
                else:
                    rows = [side[SIDE_DENSITY : SIDE_DENSITY + SY], fill]
            else:
                near, far = FORCE_ROWS + q * WX + x, UP_ROWS + q * WX + x
                own = q * CELLS + x * WY
                rows = [below[near : near + 1], moment[own : own + WY], above[near : near + 1], above[far : far + 1], fill]
            known.append(jnp.concatenate(rows, axis=0) if len(rows) > 1 else rows[0])
        flow, gained = collide(known[0], known[1:], pull)
        for c in range(3):
            speeds[c].append(flow[c])
        for q in range(19):
            step_x, step_y, _ = lattice_speeds[q]
            x_to = x + step_x
            if x_to not in (0, 1, 2, 14, 15) or (x == 15 and step_x == 1) or x == 17:
                continue
            own = q * CELLS + x * WY
            if x in (-1, 16):
                at = SIDE_POP + (UP_X if x < 0 else DOWN_X).index(q) * 4
                value = side[at : at + 4]
            elif step_y == 0:
                value = pop[own : own + 4]
            elif step_y == 1:
                at = POP_ROWS + UP_Y.index(q) * WX + x
                value = jnp.concatenate([below[at : at + 1], pop[own : own + 3]], axis=0)
            else:
                at = POP_ROWS + DOWN_Y.index(q) * WX + x
                value = jnp.concatenate([pop[own + 1 : own + 4], above[at : at + 1]], axis=0)
            post = moved_z(left * value + gained(q)[1 - step_y : 5 - step_y], q)
            if x_to < 3:
                low_side[q, x_to] = post
            else:
                high_side[q, x_to - 14] = post
    for q in range(19):
        for n, x in enumerate(KEPT[lattice_speeds[q][0]]):
            if x < 3:
                low_side[q, x] = kept[q, n]
            else:
                high_side[q, x - 14] = kept[q, n]
    copies = [
        pltpu.make_async_copy(low_side, fresh.at[:, 0:3], sent.at[0]),
        pltpu.make_async_copy(high_side, fresh.at[:, 14:16], sent.at[1]),
    ]
    for copy in copies:
        copy.start()
    for c in range(3):
        total = sample(jnp.concatenate(speeds[c], axis=0), plane[...], z_high[...], z_low[...])
        sampled[c : c + 1] = part[c : c + 1] + total
    last = pltpu.make_async_copy(sampled, sampled_far, sent.at[2])
    last.start()
    for copy in copies:
        copy.wait()
    last.wait()


def call(kernel, outputs, scratch, name, operands, cost=None):
    return pl.pallas_call(
        kernel,
        out_shape=[jax.ShapeDtypeStruct(shape, kind) for shape, kind in outputs],
        in_specs=[pl.BlockSpec(memory_space=pltpu.VMEM)] * len(operands),
        out_specs=[pl.BlockSpec(memory_space=pltpu.VMEM)] * len(outputs),
        scratch_shapes=scratch,
        compiler_params=pltpu.CompilerParams(vmem_limit_bytes=32 * 1024 * 1024),
        name=name,
        cost_estimate=cost,
    )(*operands)


def shift(value, axis, step):
    size = lax.axis_size(axis)
    return lax.ppermute(value, axis, [(i, (i + step) % size) for i in range(size)])


def per_device(populations, vert_base, vert_frac, edges, stiffness, rest):
    pop = populations.reshape(19 * CELLS, NZ)
    cost = pl.CostEstimate(flops=1 << 30, bytes_accessed=1 << 23, transcendentals=0)
    (row,) = call(rows_kernel, [((TILE, NZ), jnp.int32)], [], "rows", [], cost)
    lanes, marks, inner_plane, rim_plane = call(
        spread_kernel,
        [((SY * SX, NZ), f32), ((8, NZ), f32), ((SY * WX, VERTS), f32), ((48, VERTS), f32)],
        [],
        "spread",
        [vert_base, vert_frac, edges, stiffness.reshape(EDGES // NZ, NZ), rest, row],
    )
    moment, edge, up, down = call(
        strips_kernel,
        [((4 * CELLS, NZ), f32), ((48, NZ), f32), ((STRIP_ROWS, NZ), f32), ((STRIP_ROWS, NZ), f32)],
        [],
        "strips",
        [pop, lanes, marks],
    )
    below = shift(up, "gy", 1)
    above = shift(down, "gy", -1)
    force, z_high, z_low = call(
        tables_kernel,
        [((SY * 3 * SX, NZ), f32), ((NZ, VERTS), bf16), ((NZ, VERTS), bf16)],
        [],
        "tables",
        [vert_base, vert_frac, lanes, marks],
        cost,
    )
    right, left = call(
        merge_kernel,
        [((SIDE_ROWS, NZ), f32), ((SIDE_ROWS, NZ), f32)],
        [pltpu.VMEM((24, NZ), f32)],
        "merge",
        [force, moment, edge, below, above],
    )
    west = shift(right, "gx", 1)
    east = shift(left, "gx", -1)
    fresh, kept, part, force = call(
        inner_kernel,
        [
            ((19 * CELLS, NZ), f32),
            ((19, 2, WY, NZ), f32),
            ((3, VERTS), f32),
            ((SY * 3 * SX, NZ), f32),
        ],
        [pltpu.VMEM((3 * SY * WX, NZ), f32)],
        "inner",
        [pop, force, moment, below, above, inner_plane, z_high, z_low],
        cost,
    )
    vmem = pl.BlockSpec(memory_space=pltpu.VMEM)
    far = pl.BlockSpec(memory_space=pltpu.HBM)
    return pl.pallas_call(
        rim_kernel,
        out_shape=[
            jax.ShapeDtypeStruct((19, WX, WY, NZ), f32),
            jax.ShapeDtypeStruct((3, VERTS), f32),
        ],
        in_specs=[far] + [vmem] * 12,
        out_specs=[far, far],
        scratch_shapes=[
            pltpu.VMEM((19, 3, WY, NZ), f32),
            pltpu.VMEM((19, 2, WY, NZ), f32),
            pltpu.VMEM((3, VERTS), f32),
            pltpu.SemaphoreType.DMA((3,)),
        ],
        input_output_aliases={0: 0},
        compiler_params=pltpu.CompilerParams(vmem_limit_bytes=32 * 1024 * 1024),
        name="rim",
    )(
        fresh.reshape(19, WX, WY, NZ),
        kept,
        part,
        pop,
        force,
        moment,
        below,
        above,
        west,
        east,
        rim_plane,
        z_high,
        z_low,
    )


def solution(mesh):
    placed = (
        P(None, "gx", "gy", None),
        P(None, ("gx", "gy")),
        P(None, ("gx", "gy")),
        P(None, ("gx", "gy")),
        P(("gx", "gy")),
        P(None, ("gx", "gy")),
    )
    return jax.shard_map(
        per_device,
        mesh=mesh,
        in_specs=placed,
        out_specs=(P(None, "gx", "gy", None), P(None, ("gx", "gy"))),
        check_vma=False,
    )
```
